32 devices in a mesh: depth: 8 (over z, y), xr: 4 (over x, core).
Axes of the slice: x: 2, y: 2, z: 4, core: 2. Of those that a mesh axis runs over, the one named last changes fastest.
Arguments:
- sound_field: float32 [2, 512, 3584], P(None, 'depth', 'xr'), may hold values from -6 to 6
- index_start: float32 [512, 3584], P('depth', 'xr'), may hold values from 0.8 to 0.98
- index_end: float32 [512, 3584], P('depth', 'xr'), may hold values from 0.8 to 0.98
Outputs:
- stepped: float32 [2, 512, 3584], P(None, ('depth', 'xr'))
The draws below stay inside these ranges and needn't reach their ends.
All inputs are finite; a program needn't handle non-finite values.
Results may differ from the reference program's by a relative error of at most 0.00035.
Values sent between devices are 32-bit elements; how exact they have to be, the bound alone decides.
A program may use at most 128 MiB of HBM per device.

```python
import jax
import jax.numpy as jnp
from jax import lax

NZ = 512
NY = 3584


def shard_levels(own_key, dims, pieces, low, high):
    def one(axis_at, shards_of):
        steps = jax.random.uniform(jax.random.fold_in(jax.random.fold_in(own_key, 6), axis_at), (shards_of,), jnp.float32, low / len(pieces), high / len(pieces))
        return jnp.repeat(jnp.exp(steps), dims[axis_at] // shards_of).reshape((-1,) + (1,) * (len(dims) - axis_at - 1))

    factor_of = one(*pieces[0])
    for cut in pieces[1:]:
        factor_of = factor_of * one(*cut)
    return factor_of


def noise(stream_key, extent, spread, reach, pieces=(), dtype=jnp.bfloat16):
    result = jax.random.normal(stream_key, extent, jnp.float32) * spread
    if len(pieces) > 0:
        result = shard_levels(stream_key, extent, pieces, -0.22, 0.18) * result
    return jnp.clip(result, min=-reach, max=reach).astype(dtype)


def setup_inputs(seed: int = 0) -> dict:
    streams_of = jax.random.split(jax.random.key(seed), 4)
    sound_field = noise(streams_of[0], (2, NZ, NY), 1.0, 6.0, ((1, 8), (2, 4)), jnp.float32)
    index_start = jnp.clip(0.8 + 0.18 * jax.random.uniform(streams_of[1], (NZ, NY), jnp.float32) ** shard_levels(streams_of[1], (NZ, NY), ((0, 8), (1, 4)), -0.2, 0.2), 0.8, 0.98)
    index_end = jnp.clip(0.8 + 0.18 * jax.random.uniform(streams_of[2], (NZ, NY), jnp.float32) ** shard_levels(streams_of[2], (NZ, NY), ((0, 8), (1, 4)), -0.2, 0.2), 0.8, 0.98)
    return {"sound_field": sound_field, "index_start": index_start, "index_end": index_end}


depth_stiffness = 1.6
cross_stiffness = 1.2
numer_re = 2.857
numer_im = 0.004
denom_re = 2.857
denom_im = -0.004


def complex_multiply(left_re, left_im, right_re, right_im):
    return left_re * right_re - left_im * right_im, left_re * right_im + left_im * right_re


def complex_divide(left_re, left_im, right_re, right_im):
    modulus = right_re * right_re + right_im * right_im
    return (left_re * right_re + left_im * right_im) / modulus, (left_im * right_re - left_re * right_im) / modulus


def explicit_part(values, potential, stiffness):
    border = jnp.zeros_like(values[:1])
    padded = jnp.concatenate([border, values, border], axis=0)
    return stiffness * (padded[:-2] - 2.0 * values + padded[2:]) + potential * values


def right_side(value_re, value_im, potential, stiffness):
    product_real, product_imaginary = complex_multiply(numer_re, numer_im, explicit_part(value_re, potential, stiffness), explicit_part(value_im, potential, stiffness))
    return value_re + product_real, value_im + product_imaginary


def line_solve(forcing_real, forcing_imaginary, potential, stiffness):
    offdiagonal_real = denom_re * stiffness
    offdiagonal_imaginary = denom_im * stiffness
    diagonal_real = 1.0 + denom_re * (potential - 2.0 * stiffness)
    diagonal_imaginary = denom_im * (potential - 2.0 * stiffness)

    def forward_sweep(carry_state, input_arrays):
        eliminator_real, eliminator_imaginary, filler_real, filler_imaginary = carry_state
        dgr, dgi, src_re, src_im = input_arrays
        subdiagonal_real, subdiagonal_imaginary = complex_multiply(offdiagonal_real, offdiagonal_imaginary, eliminator_real, eliminator_imaginary)
        pivot_value_real = dgr - subdiagonal_real
        pivot_value_imaginary = dgi - subdiagonal_imaginary
        updated_eliminator = complex_divide(offdiagonal_real, offdiagonal_imaginary, pivot_value_real, pivot_value_imaginary)
        carried_re, carried_im = complex_multiply(offdiagonal_real, offdiagonal_imaginary, filler_real, filler_imaginary)
        updated_filler = complex_divide(src_re - carried_re, src_im - carried_im, pivot_value_real, pivot_value_imaginary)
        sweep_result = (updated_eliminator[0], updated_eliminator[1], updated_filler[0], updated_filler[1])
        return sweep_result, sweep_result

    empty_line_row = jnp.zeros_like(forcing_real[0])
    start_row = (empty_line_row, empty_line_row, empty_line_row, empty_line_row)
    unused_item, (eliminator_real, eliminator_imaginary, filler_real, filler_imaginary) = lax.scan(forward_sweep, start_row, (diagonal_real, diagonal_imaginary, forcing_real, forcing_imaginary))

    def backward_sweep(carry_state, input_arrays):
        following_real, following_imaginary = carry_state
        cell_eliminator_real, cell_eliminator_imaginary, cell_filler_real, cell_filler_imaginary = input_arrays
        product_real, product_imaginary = complex_multiply(cell_eliminator_real, cell_eliminator_imaginary, following_real, following_imaginary)
        sweep_result = (cell_filler_real - product_real, cell_filler_imaginary - product_imaginary)
        return sweep_result, sweep_result

    unused_item, (unknown_real, unknown_imaginary) = lax.scan(backward_sweep, (empty_line_row, empty_line_row), (eliminator_real, eliminator_imaginary, filler_real, filler_imaginary), reverse=True)
    return unknown_real, unknown_imaginary


def reference(sound_field, index_start, index_end):
    depth_potential = (index_start - 1.0) * 0.5
    cross_potential = (index_end - 1.0) * 0.5
    forcing_real, forcing_imaginary = right_side(sound_field[0], sound_field[1], depth_potential, depth_stiffness)
    middle_re, middle_im = line_solve(forcing_real, forcing_imaginary, depth_potential, depth_stiffness)
    cross_re, cross_im = right_side(middle_re.T, middle_im.T, cross_potential.T, cross_stiffness)
    final_re, final_im = line_solve(cross_re, cross_im, cross_potential.T, cross_stiffness)
    return jnp.stack([final_re.T, final_im.T])
```

```python
import functools

import jax
import jax.numpy as jnp
from jax import lax
from jax.experimental import pallas as pl
from jax.experimental.pallas import tpu as pltpu
from jax.sharding import PartitionSpec as P
import numpy as np

depth_stiffness = 1.6
cross_stiffness = 1.2
numer = 2.857 + 0.004j
denom = 2.857 - 0.004j
LANES = 128
SUBLANES = 8
SUMMARY_ROWS = 16
MESH = pl.DeviceIdType.MESH


class Line:
    def __init__(self, stiffness):
        shift = 1.0 / denom
        self.slope = -0.5 / stiffness
        self.level = 2.0 - shift.real / stiffness + 0.5 / stiffness
        self.damping = shift.imag / stiffness
        cosine = 0.5 * (self.level + self.slope * 0.89)
        angle = float(np.arccos(cosine))
        self.mu = complex(np.exp(0.5j * angle))
        self.nu = self.mu.conjugate()
        self.inv_det = 1.0 / (self.nu * self.nu - self.mu * self.mu)
        self.wall = -self.mu * self.mu
        self.alpha = numer / denom
        self.beta = (denom - numer) / (denom * denom * stiffness)


def mul(x, y):
    return (x[0] * y[0] - x[1] * y[1], x[0] * y[1] + x[1] * y[0])


def add(x, y):
    return (x[0] + y[0], x[1] + y[1])


def sub(x, y):
    return (x[0] - y[0], x[1] - y[1])


def cmul(c, x):
    c = complex(c)
    return (c.real * x[0] - c.imag * x[1], c.real * x[1] + c.imag * x[0])


def recip(x):
    scale = 1.0 / (x[0] * x[0] + x[1] * x[1])
    return (x[0] * scale, -x[1] * scale)


def one_minus(x):
    return (1.0 - x[0], -x[1])


def cmap(fn, x):
    return (fn(x[0]), fn(x[1]))


def step(line, coef, here, before, force=None):
    real = coef * here[0] + line.damping * here[1] - before[0]
    imag = coef * here[1] - line.damping * here[0] - before[1]
    if force is not None:
        real, imag = real + force[0], imag + force[1]
    return (real, imag)


def coefficient(line, index):
    return line.level + line.slope * index


def segment_medium(line, coefs):
    shape = coefs[0].shape
    def const(c):
        return (jnp.full(shape, c.real, jnp.float32), jnp.full(shape, c.imag, jnp.float32))
    p0, p1 = const(line.nu), const(line.mu)
    q0, q1 = const(line.mu), const(line.nu)
    for coef in coefs:
        p0, p1 = p1, step(line, coef, p1, p0)
        q0, q1 = q1, step(line, coef, q1, q0)
    lower, upper = -line.mu * line.inv_det, line.nu * line.inv_det
    t21 = add(cmul(lower, p0), cmul(upper, p1))
    t22 = add(cmul(lower, q0), cmul(upper, q1))
    t12 = add(cmul(upper, q0), cmul(lower, q1))
    t = recip(t22)
    r1 = mul(t21, t)
    r1 = (-r1[0], -r1[1])
    r2 = mul(t12, t)
    return t, r1, r2


def segment_source(line, coefs, forces, t, r2):
    zero = jnp.zeros(coefs[0].shape, jnp.float32)
    v0, v1 = (zero, zero), (zero, zero)
    for position, (coef, force) in enumerate(zip(coefs, forces)):
        if position == 0:
            v0, v1 = v1, force
        else:
            v0, v1 = v1, step(line, coef, v1, v0, force)
    lower, upper = -line.mu * line.inv_det, line.nu * line.inv_det
    right = add(cmul(upper, v0), cmul(lower, v1))
    left = add(cmul(lower, v0), cmul(upper, v1))
    s1 = mul(left, t)
    s1 = (-s1[0], -s1[1])
    s2 = sub(right, mul(r2, left))
    return s1, s2


def from_right(x, axis, amount):
    return cmap(lambda v: pltpu.roll(v, v.shape[axis] - amount, axis), x)


def from_left(x, axis, amount):
    return cmap(lambda v: pltpu.roll(v, amount, axis), x)


def medium_level(medium, axis, amount):
    t_a, r1_a, r2_a = medium
    t_b, r1_b, r2_b = (from_right(v, axis, amount) for v in medium)
    d = recip(one_minus(mul(r2_a, r1_b)))
    ra, rb = mul(d, r2_a), mul(d, r1_b)
    tad, tbd = mul(t_a, d), mul(t_b, d)
    x1, x2 = mul(t_a, rb), mul(t_b, ra)
    merged = (mul(tad, t_b), add(r1_a, mul(x1, t_a)), add(r2_b, mul(x2, t_b)))
    return merged, (d, ra, rb, t_a, t_b, tad, tbd, x1, x2)


def source_level(kept, source, axis, amount):
    d, ra, rb, t_a, t_b, tad, tbd, x1, x2 = kept
    s1_a, s2_a = source
    s1_b, s2_b = (from_right(v, axis, amount) for v in source)
    e_p = add(mul(d, s2_a), mul(ra, s1_b))
    e_q = add(mul(d, s1_b), mul(rb, s2_a))
    merged = (add(s1_a, mul(t_a, e_q)), add(s2_b, mul(t_b, e_p)))
    return merged, (e_p, e_q)


def down_level(kept, inner, p_left, q_right, axis, amount, unit):
    d, ra, rb, t_a, t_b, tad, tbd, x1, x2 = kept
    p_mid = add(add(mul(tad, p_left), mul(x2, q_right)), inner[0])
    q_mid = add(add(mul(x1, p_left), mul(tbd, q_right)), inner[1])
    shape = p_left[0].shape
    place = lax.broadcasted_iota(jnp.int32, shape, axis)
    is_left = (place % (2 * amount)) < amount
    p_moved = from_left(p_mid, axis, amount)
    q_moved = from_left(q_right, axis, amount)
    p_new = tuple(jnp.where(is_left, a, b) for a, b in zip(p_left, p_moved))
    q_new = tuple(jnp.where(is_left, a, b) for a, b in zip(q_mid, q_moved))
    return p_new, q_new


def medium_tree(medium, axis, count, unit=1):
    levels = []
    amount = unit
    while amount < count * unit:
        medium, kept = medium_level(medium, axis, amount)
        levels.append((amount, kept))
        amount *= 2
    return medium, levels


def source_tree(levels, source, axis):
    inners = []
    for amount, kept in levels:
        source, inner = source_level(kept, source, axis, amount)
        inners.append(inner)
    return source, inners


def down_tree(levels, inners, p_left, q_right, axis):
    for (amount, kept), inner in zip(reversed(levels), reversed(inners)):
        p_left, q_right = down_level(kept, inner, p_left, q_right, axis, amount, 1)
    return p_left, q_right


def between_walls(line, medium, source):
    t, r1, r2 = medium
    s1, s2 = source
    tw = cmul(line.wall, t)
    first = one_minus(cmul(line.wall, r1))
    second = one_minus(cmul(line.wall, r2))
    scale = recip(sub(mul(first, second), mul(tw, tw)))
    q_left = mul(scale, add(mul(second, s1), mul(tw, s2)))
    p_right = mul(scale, add(mul(tw, s1), mul(first, s2)))
    return cmul(line.wall, q_left), cmul(line.wall, p_right)


def segment_start(line, medium, source, p_left, q_right):
    t, r1, r2 = medium
    q_left = add(add(mul(r1, p_left), mul(t, q_right)), source[0])
    before = add(cmul(line.nu, p_left), cmul(line.mu, q_left))
    here = add(cmul(line.mu, p_left), cmul(line.nu, q_left))
    return before, here


def result(line, force, here):
    return add(cmul(line.alpha, force), cmul(line.beta, here))


def kernel(
    nd, nx, field, start, end, out,
    summary, gathered, answer, boundary, middle, received, end_received,
    tall_end, tall_field, tall_out,
    sum_send, sum_recv, ans_send, ans_recv, end_send, end_recv, mid_send, mid_recv,
):
    rows, width = start.shape[1], start.shape[0] * LANES
    tiles = width // LANES
    cells = rows // SUBLANES
    out_rows = rows // nx
    dep = lax.axis_index("depth")
    xr = lax.axis_index("xr")
    depth_line = Line(depth_stiffness)
    cross_line = Line(cross_stiffness)

    barrier = pltpu.get_barrier_semaphore()

    @pl.loop(1, nd)
    def _(offset):
        pl.semaphore_signal(barrier, 1, device_id=(lax.rem(dep + offset, nd), xr), device_id_type=MESH)

    @pl.loop(1, nx)
    def _(offset):
        pl.semaphore_signal(barrier, 1, device_id=(dep, lax.rem(xr + offset, nx)), device_id_type=MESH)

    pl.semaphore_wait(barrier, nd - 1 + nx - 1)

    def end_copy(peer, source_block):
        return pltpu.make_async_remote_copy(
            src_ref=end.at[:, pl.ds(pl.multiple_of(peer * out_rows, out_rows), out_rows), :],
            dst_ref=end_received.at[source_block],
            send_sem=end_send.at[peer],
            recv_sem=end_recv.at[source_block],
            device_id=(dep, peer),
            device_id_type=MESH,
        )

    for offset in range(1, nx):
        end_copy(lax.rem(xr + offset, nx), xr).start()

    def strided(ref, *lead):
        return [
            jnp.concatenate(
                [ref[(tile,) + lead + (pl.ds(cell, SUBLANES, stride=cells), slice(None))] for tile in range(tiles)],
                axis=1,
            )
            for cell in range(cells)
        ]

    def depth_coefs():
        return [coefficient(depth_line, v) for v in strided(start)]

    coefs = depth_coefs()
    forces = list(zip(strided(field, 0), strided(field, 1)))
    medium = segment_medium(depth_line, coefs)
    source = segment_source(depth_line, coefs, forces, medium[0], medium[2])
    total_medium, levels = medium_tree(medium, 0, SUBLANES)
    total_source, inners = source_tree(levels, source, 0)
    parts = [v for pair in (*total_medium, *total_source) for v in pair]
    for tile in range(tiles):
        for row, part in enumerate(parts):
            summary[tile, row : row + 1, :] = part[0:1, tile * LANES : (tile + 1) * LANES]

    def sum_copy(tile, origin):
        return pltpu.make_async_remote_copy(
            src_ref=summary.at[tile],
            dst_ref=gathered.at[pl.ds(pl.multiple_of(origin * SUMMARY_ROWS, SUMMARY_ROWS), SUMMARY_ROWS), :],
            send_sem=sum_send.at[tile],
            recv_sem=sum_recv.at[origin],
            device_id=(tile, xr),
            device_id_type=MESH,
        )

    for tile in range(tiles):

        @pl.when(dep != tile)
        def _():
            sum_copy(tile, dep).start()

    def tall(pieces):
        stacked = jnp.concatenate(pieces, axis=0)
        if stacked.shape[0] < LANES:
            pad = jnp.full((LANES - stacked.shape[0], LANES), 0.89, jnp.float32)
            stacked = jnp.concatenate([stacked, pad], axis=0)
        return stacked.T

    for tile in range(tiles):
        end_received[xr, tile] = end[tile, pl.ds(pl.multiple_of(xr * out_rows, out_rows), out_rows), :]
    for offset in range(nx):
        block = lax.rem(xr + offset, nx)
        if offset > 0:
            end_copy(xr, block).wait_recv()
        tall_end[pl.ds(pl.multiple_of(block * LANES, LANES), LANES), :] = tall(
            [end_received[block, tile] for tile in range(tiles)]
        )
    cross_cells = LANES // SUBLANES

    def tall_strided(ref, *lead):
        return [
            jnp.concatenate(
                [
                    ref[lead + (pl.ds(block * LANES + cell, SUBLANES, stride=cross_cells), slice(None))]
                    for block in range(nx)
                ],
                axis=1,
            )
            for cell in range(cross_cells)
        ]

    def cross_coefs():
        return [coefficient(cross_line, v) for v in tall_strided(tall_end)]

    cross_medium = segment_medium(cross_line, cross_coefs())

    def ans_copy(peer, tile):
        return pltpu.make_async_remote_copy(
            src_ref=answer.at[pl.ds(pl.multiple_of(peer * SUBLANES, SUBLANES), SUBLANES), :],
            dst_ref=boundary.at[tile],
            send_sem=ans_send.at[peer],
            recv_sem=ans_recv.at[tile],
            device_id=(peer, xr),
            device_id_type=MESH,
        )

    @pl.when(dep < tiles)
    def _():
        gathered[pl.ds(pl.multiple_of(dep * SUMMARY_ROWS, SUMMARY_ROWS), SUMMARY_ROWS), :] = summary[dep]
        for offset in range(1, nd):
            sum_copy(0, lax.rem(dep + offset, nd)).wait_recv()
        values = [gathered[pl.ds(row, nd, stride=SUMMARY_ROWS), :] for row in range(10)]
        pairs = [(values[2 * i], values[2 * i + 1]) for i in range(5)]
        all_medium, all_levels = medium_tree(tuple(pairs[:3]), 0, nd)
        all_source, all_inners = source_tree(all_levels, tuple(pairs[3:]), 0)
        p_all, q_all = between_walls(depth_line, all_medium, all_source)
        p_all, q_all = down_tree(all_levels, all_inners, p_all, q_all, 0)
        for row, value in enumerate((*p_all, *q_all)):
            answer[pl.ds(row, nd, stride=SUBLANES), :] = value
        boundary[dep] = answer[pl.ds(pl.multiple_of(dep * SUBLANES, SUBLANES), SUBLANES), :]
        for offset in range(1, nd):
            ans_copy(lax.rem(dep + offset, nd), dep).start()

    block_medium, block_levels = medium_tree(cross_medium, 0, SUBLANES)
    sub_place = lax.broadcasted_iota(jnp.int32, (SUBLANES, LANES), 0)
    lane_place = lax.broadcasted_iota(jnp.int32, (SUBLANES, LANES), 1)
    used = lane_place < tiles * out_rows

    def packed(value, fill):
        total = jnp.zeros((SUBLANES, LANES), jnp.float32)
        for block in range(nx):
            row = jnp.broadcast_to(value[0:1, block * LANES : (block + 1) * LANES], (SUBLANES, LANES))
            total = jnp.where(sub_place == block, row, total)
        return jnp.where(used, total, fill)

    def unpacked(value):
        return jnp.concatenate(
            [jnp.broadcast_to(value[block : block + 1, :], (SUBLANES, LANES)) for block in range(nx)], axis=1
        )

    slots = LANES // out_rows
    packed_medium = tuple(
        (packed(v[0], fill), packed(v[1], 0.0)) for v, fill in zip(block_medium, (1.0, 0.0, 0.0))
    )
    tile_medium, tile_levels = medium_tree(packed_medium, 1, slots, out_rows)
    line_medium, line_levels = medium_tree(tile_medium, 0, nx)

    for tile in range(tiles):

        @pl.when(dep != tile)
        def _():
            ans_copy(dep, tile).wait_recv()

    def incoming(row):
        return jnp.concatenate(
            [jnp.broadcast_to(boundary[tile, row : row + 1, :], (SUBLANES, LANES)) for tile in range(tiles)], axis=1
        )

    p_left, q_right = (incoming(0), incoming(1)), (incoming(2), incoming(3))
    p_left, q_right = down_tree(levels, inners, p_left, q_right, 0)
    all_before, all_here = segment_start(depth_line, medium, source, p_left, q_right)

    def mid_copy(tile, peer, source_block):
        return pltpu.make_async_remote_copy(
            src_ref=middle.at[tile, :, pl.ds(pl.multiple_of(peer * out_rows, out_rows), out_rows), :],
            dst_ref=received.at[source_block, tile],
            send_sem=mid_send.at[tile, peer],
            recv_sem=mid_recv.at[tile, source_block],
            device_id=(dep, peer),
            device_id_type=MESH,
        )

    for tile in range(tiles):
        cut = slice(tile * LANES, (tile + 1) * LANES)
        before = cmap(lambda v: v[:, cut], all_before)
        here = cmap(lambda v: v[:, cut], all_here)
        for cell in range(cells):
            place = pl.ds(cell, SUBLANES, stride=cells)
            force = (field[tile, 0, place, :], field[tile, 1, place, :])
            value = result(depth_line, force, here)
            middle[tile, 0, place, :] = value[0]
            middle[tile, 1, place, :] = value[1]
            if cell < cells - 1:
                coef = coefficient(depth_line, start[tile, place, :])
                before, here = here, step(depth_line, coef, here, before, force)
        for offset in range(1, nx):
            mid_copy(tile, lax.rem(xr + offset, nx), xr).start()

    own = pl.ds(pl.multiple_of(xr * out_rows, out_rows), out_rows)
    for tile in range(tiles):
        for c in range(2):
            received[xr, tile, c] = middle[tile, c, own, :]
    for offset in range(nx):
        block = lax.rem(xr + offset, nx)
        if offset > 0:
            for tile in range(tiles):
                mid_copy(tile, xr, block).wait_recv()
        for c in range(2):
            tall_field[c, pl.ds(pl.multiple_of(block * LANES, LANES), LANES), :] = tall(
                [received[block, tile, c] for tile in range(tiles)]
            )
    coefs = cross_coefs()
    forces = list(zip(tall_strided(tall_field, 0), tall_strided(tall_field, 1)))
    source = segment_source(cross_line, coefs, forces, cross_medium[0], cross_medium[2])
    block_source, block_inners = source_tree(block_levels, source, 0)
    packed_source = tuple((packed(v[0], 0.0), packed(v[1], 0.0)) for v in block_source)
    tile_source, tile_inners = source_tree(tile_levels, packed_source, 1)
    line_source, line_inners = source_tree(line_levels, tile_source, 0)
    p_left, q_right = between_walls(cross_line, line_medium, line_source)
    p_left, q_right = down_tree(line_levels, line_inners, p_left, q_right, 0)
    p_left, q_right = down_tree(tile_levels, tile_inners, p_left, q_right, 1)
    p_left, q_right = cmap(unpacked, p_left), cmap(unpacked, q_right)
    p_left, q_right = down_tree(block_levels, block_inners, p_left, q_right, 0)
    all_before, all_here = segment_start(cross_line, cross_medium, source, p_left, q_right)
    for block in range(nx):
        cut = slice(block * LANES, (block + 1) * LANES)
        before = cmap(lambda v: v[:, cut], all_before)
        here = cmap(lambda v: v[:, cut], all_here)
        for cell in range(cross_cells):
            place = pl.ds(block * LANES + cell, SUBLANES, stride=cross_cells)
            force = (tall_field[0, place, :], tall_field[1, place, :])
            value = result(cross_line, force, here)
            tall_out[0, place, :] = value[0]
            tall_out[1, place, :] = value[1]
            if cell < cross_cells - 1:
                coef = coefficient(cross_line, tall_end[place, :])
                before, here = here, step(cross_line, coef, here, before, force)
        for c in range(2):
            flat = tall_out[c, block * LANES : (block + 1) * LANES, :].T
            for tile in range(tiles):
                at = block * width + tile * LANES
                out[c, :, at : at + LANES] = flat[tile * out_rows : (tile + 1) * out_rows, :]

    for offset in range(1, nx):
        peer = lax.rem(xr + offset, nx)
        end_copy(peer, xr).wait_send()
        for tile in range(tiles):
            mid_copy(tile, peer, xr).wait_send()
    for tile in range(tiles):

        @pl.when(dep != tile)
        def _():
            sum_copy(tile, dep).wait_send()

    @pl.when(dep < tiles)
    def _():
        for offset in range(1, nd):
            ans_copy(lax.rem(dep + offset, nd), dep).wait_send()


def local(nd, nx, sound_field, index_start, index_end):
    rows, width = index_start.shape
    tiles = width // LANES
    out_rows = rows // nx
    assert tiles <= nd and tiles * out_rows <= LANES and nx <= SUBLANES
    field = sound_field.reshape(2, rows, tiles, LANES).transpose(2, 0, 1, 3)
    start = index_start.reshape(rows, tiles, LANES).transpose(1, 0, 2)
    end = index_end.reshape(rows, tiles, LANES).transpose(1, 0, 2)
    f32 = jnp.float32
    dma = pltpu.SemaphoreType.DMA
    return pl.pallas_call(
        functools.partial(kernel, nd, nx),
        out_shape=jax.ShapeDtypeStruct((2, out_rows, width * nx), f32),
        in_specs=[pl.BlockSpec(memory_space=pltpu.VMEM)] * 3,
        out_specs=pl.BlockSpec(memory_space=pltpu.VMEM),
        scratch_shapes=[
            pltpu.VMEM((tiles, SUMMARY_ROWS, LANES), f32),
            pltpu.VMEM((nd * SUMMARY_ROWS, LANES), f32),
            pltpu.VMEM((nd * SUBLANES, LANES), f32),
            pltpu.VMEM((tiles, SUBLANES, LANES), f32),
            pltpu.VMEM((tiles, 2, rows, LANES), f32),
            pltpu.VMEM((nx, tiles, 2, out_rows, LANES), f32),
            pltpu.VMEM((nx, tiles, out_rows, LANES), f32),
            pltpu.VMEM((nx * LANES, LANES), f32),
            pltpu.VMEM((2, nx * LANES, LANES), f32),
            pltpu.VMEM((2, nx * LANES, LANES), f32),
            dma((tiles,)),
            dma((nd,)),
            dma((nd,)),
            dma((tiles,)),
            dma((nx,)),
            dma((nx,)),
            dma((tiles, nx)),
            dma((tiles, nx)),
        ],
        compiler_params=pltpu.CompilerParams(
            collective_id=0, has_side_effects=True, vmem_limit_bytes=32 * 1024 * 1024
        ),
        cost_estimate=pl.CostEstimate(flops=20_000_000, bytes_accessed=2_000_000, transcendentals=0),
    )(field, start, end)


def solution(mesh):
    nd, nx = mesh.shape["depth"], mesh.shape["xr"]
    in_specs = (P(None, "depth", "xr"), P("depth", "xr"), P("depth", "xr"))
    out_specs = P(None, ("depth", "xr"), None)
    return jax.shard_map(
        functools.partial(local, nd, nx), mesh=mesh, in_specs=in_specs, out_specs=out_specs, check_vma=False
    )
```

```python
import functools

import jax
import jax.numpy as jnp
from jax import lax
from jax.experimental import pallas as pl
from jax.experimental.pallas import tpu as pltpu
from jax.sharding import PartitionSpec as P
import numpy as np

depth_stiffness = 1.6
cross_stiffness = 1.2
numer = 2.857 + 0.004j
denom = 2.857 - 0.004j
LANES = 128
SUBLANES = 8
SUMMARY_ROWS = 16
MESH = pl.DeviceIdType.MESH


class Line:
    def __init__(self, stiffness):
        shift = 1.0 / denom
        self.slope = -0.5 / stiffness
        self.level = 2.0 - shift.real / stiffness + 0.5 / stiffness
        self.damping = shift.imag / stiffness
        cosine = 0.5 * (self.level + self.slope * 0.89)
        angle = float(np.arccos(cosine))
        self.mu = complex(np.exp(0.5j * angle))
        self.nu = self.mu.conjugate()
        self.inv_det = 1.0 / (self.nu * self.nu - self.mu * self.mu)
        self.wall = -self.mu * self.mu
        self.alpha = numer / denom
        self.beta = (denom - numer) / (denom * denom * stiffness)


def mul(x, y):
    return (x[0] * y[0] - x[1] * y[1], x[0] * y[1] + x[1] * y[0])


def add(x, y):
    return (x[0] + y[0], x[1] + y[1])


def sub(x, y):
    return (x[0] - y[0], x[1] - y[1])


def cmul(c, x):
    c = complex(c)
    return (c.real * x[0] - c.imag * x[1], c.real * x[1] + c.imag * x[0])


def recip(x):
    scale = 1.0 / (x[0] * x[0] + x[1] * x[1])
    return (x[0] * scale, -x[1] * scale)


def one_minus(x):
    return (1.0 - x[0], -x[1])


def cmap(fn, x):
    return (fn(x[0]), fn(x[1]))


def step(line, coef, here, before, force=None):
    real = coef * here[0] + line.damping * here[1] - before[0]
    imag = coef * here[1] - line.damping * here[0] - before[1]
    if force is not None:
        real, imag = real + force[0], imag + force[1]
    return (real, imag)


def coefficient(line, index):
    return line.level + line.slope * index


def segment_medium(line, coefs):
    shape = coefs[0].shape
    def const(c):
        return (jnp.full(shape, c.real, jnp.float32), jnp.full(shape, c.imag, jnp.float32))
    p0, p1 = const(line.nu), const(line.mu)
    q0, q1 = const(line.mu), const(line.nu)
    for coef in coefs:
        p0, p1 = p1, step(line, coef, p1, p0)
        q0, q1 = q1, step(line, coef, q1, q0)
    lower, upper = -line.mu * line.inv_det, line.nu * line.inv_det
    t21 = add(cmul(lower, p0), cmul(upper, p1))
    t22 = add(cmul(lower, q0), cmul(upper, q1))
    t12 = add(cmul(upper, q0), cmul(lower, q1))
    t = recip(t22)
    r1 = mul(t21, t)
    r1 = (-r1[0], -r1[1])
    r2 = mul(t12, t)
    return t, r1, r2


def segment_source(line, coefs, forces, t, r2):
    zero = jnp.zeros(coefs[0].shape, jnp.float32)
    v0, v1 = (zero, zero), (zero, zero)
    for position, (coef, force) in enumerate(zip(coefs, forces)):
        if position == 0:
            v0, v1 = v1, force
        else:
            v0, v1 = v1, step(line, coef, v1, v0, force)
    lower, upper = -line.mu * line.inv_det, line.nu * line.inv_det
    right = add(cmul(upper, v0), cmul(lower, v1))
    left = add(cmul(lower, v0), cmul(upper, v1))
    s1 = mul(left, t)
    s1 = (-s1[0], -s1[1])
    s2 = sub(right, mul(r2, left))
    return s1, s2


def from_right(x, axis, amount):
    return cmap(lambda v: pltpu.roll(v, v.shape[axis] - amount, axis), x)


def from_left(x, axis, amount):
    return cmap(lambda v: pltpu.roll(v, amount, axis), x)


def merge_medium(left, right):
    t_a, r1_a, r2_a = left
    t_b, r1_b, r2_b = right
    d = recip(one_minus(mul(r2_a, r1_b)))
    ra, rb = mul(d, r2_a), mul(d, r1_b)
    tad, tbd = mul(t_a, d), mul(t_b, d)
    x1, x2 = mul(t_a, rb), mul(t_b, ra)
    merged = (mul(tad, t_b), add(r1_a, mul(x1, t_a)), add(r2_b, mul(x2, t_b)))
    return merged, (d, ra, rb, t_a, t_b, tad, tbd, x1, x2)


def merge_source(kept, left, right):
    d, ra, rb, t_a, t_b, tad, tbd, x1, x2 = kept
    s1_a, s2_a = left
    s1_b, s2_b = right
    e_p = add(mul(d, s2_a), mul(ra, s1_b))
    e_q = add(mul(d, s1_b), mul(rb, s2_a))
    merged = (add(s1_a, mul(t_a, e_q)), add(s2_b, mul(t_b, e_p)))
    return merged, (e_p, e_q)


def middle_waves(kept, inner, p_left, q_right):
    d, ra, rb, t_a, t_b, tad, tbd, x1, x2 = kept
    p_mid = add(add(mul(tad, p_left), mul(x2, q_right)), inner[0])
    q_mid = add(add(mul(x1, p_left), mul(tbd, q_right)), inner[1])
    return p_mid, q_mid


def medium_list(items):
    levels = []
    while len(items) > 1:
        pairs = [merge_medium(a, b) for a, b in zip(items[0::2], items[1::2])]
        items = [merged for merged, _ in pairs]
        levels.append([kept for _, kept in pairs])
    return items[0], levels


def source_list(levels, items):
    inners = []
    for level in levels:
        pairs = [merge_source(kept, a, b) for kept, a, b in zip(level, items[0::2], items[1::2])]
        items = [merged for merged, _ in pairs]
        inners.append([inner for _, inner in pairs])
    return items[0], inners


def down_list(levels, inners, p_left, q_right):
    waves = [(p_left, q_right)]
    for level, inner_level in zip(reversed(levels), reversed(inners)):
        finer = []
        for kept, inner, (p, q) in zip(level, inner_level, waves):
            p_mid, q_mid = middle_waves(kept, inner, p, q)
            finer += [(p, q_mid), (p_mid, q)]
        waves = finer
    return waves


def medium_level(medium, axis, amount):
    return merge_medium(medium, tuple(from_right(v, axis, amount) for v in medium))


def source_level(kept, source, axis, amount):
    return merge_source(kept, source, tuple(from_right(v, axis, amount) for v in source))


def down_level(kept, inner, p_left, q_right, axis, amount):
    p_mid, q_mid = middle_waves(kept, inner, p_left, q_right)
    shape = p_left[0].shape
    place = lax.broadcasted_iota(jnp.int32, shape, axis)
    is_left = (place % (2 * amount)) < amount
    p_moved = from_left(p_mid, axis, amount)
    q_moved = from_left(q_right, axis, amount)
    p_new = tuple(jnp.where(is_left, a, b) for a, b in zip(p_left, p_moved))
    q_new = tuple(jnp.where(is_left, a, b) for a, b in zip(q_mid, q_moved))
    return p_new, q_new


def medium_tree(medium, axis, count, unit=1):
    levels = []
    amount = unit
    while amount < count * unit:
        medium, kept = medium_level(medium, axis, amount)
        levels.append((amount, kept))
        amount *= 2
    return medium, levels


def source_tree(levels, source, axis):
    inners = []
    for amount, kept in levels:
        source, inner = source_level(kept, source, axis, amount)
        inners.append(inner)
    return source, inners


def down_tree(levels, inners, p_left, q_right, axis):
    for (amount, kept), inner in zip(reversed(levels), reversed(inners)):
        p_left, q_right = down_level(kept, inner, p_left, q_right, axis, amount)
    return p_left, q_right


def between_walls(line, medium, source):
    t, r1, r2 = medium
    s1, s2 = source
    tw = cmul(line.wall, t)
    first = one_minus(cmul(line.wall, r1))
    second = one_minus(cmul(line.wall, r2))
    scale = recip(sub(mul(first, second), mul(tw, tw)))
    q_left = mul(scale, add(mul(second, s1), mul(tw, s2)))
    p_right = mul(scale, add(mul(tw, s1), mul(first, s2)))
    return cmul(line.wall, q_left), cmul(line.wall, p_right)


def segment_start(line, medium, source, p_left, q_right):
    t, r1, r2 = medium
    q_left = add(add(mul(r1, p_left), mul(t, q_right)), source[0])
    before = add(cmul(line.nu, p_left), cmul(line.mu, q_left))
    here = add(cmul(line.mu, p_left), cmul(line.nu, q_left))
    return before, here


def result(line, force, here):
    return add(cmul(line.alpha, force), cmul(line.beta, here))


def kernel(
    nd, nx, field, start, end, out,
    own, received, summary, gathered, answer, boundary, edge_out, edge_in,
    middle, tall_end, tall_field, tall_out,
    sum_send, sum_recv, ans_send, ans_recv, bulk_send, bulk_recv, edge_send, edge_recv,
):
    used_rows = start.shape[1]
    width = out.shape[2] // nx
    tiles = width // LANES
    out_rows = out.shape[1]
    slots = LANES // out_rows
    dep = lax.axis_index("depth")
    xr = lax.axis_index("xr")
    depth_line = Line(depth_stiffness)
    cross_line = Line(cross_stiffness)

    barrier = pltpu.get_barrier_semaphore()

    @pl.loop(1, nd)
    def _(offset):
        pl.semaphore_signal(barrier, 1, device_id=(lax.rem(dep + offset, nd), xr), device_id_type=MESH)

    @pl.loop(1, nx)
    def _(offset):
        pl.semaphore_signal(barrier, 1, device_id=(dep, lax.rem(xr + offset, nx)), device_id_type=MESH)

    def peer_at(offset):
        base = xr // 2 * 2
        return lax.rem(base + 2 * (offset // 2), nx) + lax.rem(xr + offset, 2)

    RE, IM, START, END = range(4)

    def at(block, part):
        return pl.multiple_of((block * 4 + part) * LANES, LANES)

    def bulk_copy(peer, source_block, part):
        source_ref = field.at[peer, part] if part < 2 else (start if part == START else end).at[peer]
        return pltpu.make_async_remote_copy(
            src_ref=source_ref,
            dst_ref=received.at[pl.ds(at(source_block, part), used_rows), :],
            send_sem=bulk_send.at[peer, part],
            recv_sem=bulk_recv.at[source_block, part],
            device_id=(dep, peer),
            device_id_type=MESH,
        )

    far_first = list(range(2, nx)) + [1]
    pl.semaphore_wait(barrier, nd - 1 + nx - 1)
    for part in (END, START, RE, IM):
        for offset in far_first:
            bulk_copy(peer_at(offset), xr, part).start()

    for block in range(nx):
        for part in range(4):
            base = (block * 4 + part) * LANES
            if used_rows < LANES:
                pad = jnp.full((LANES - used_rows, LANES), 0.0 if part < 2 else 0.89, jnp.float32)
                received[base + used_rows : base + LANES, :] = pad
                if part < 3:
                    own[base + used_rows : base + LANES, :] = pad
            if part < 3:
                own[base : base + used_rows, :] = field[block, part] if part < 2 else start[block]
    for part in range(4):
        received[pl.ds(at(xr, part), used_rows), :] = field[xr, part] if part < 2 else (start if part == START else end)[xr]

    def wide(ref, part, row):
        return jnp.concatenate(
            [ref[pl.ds((block * 4 + part) * LANES + row, slots, stride=out_rows), :] for block in range(nx)], axis=1
        )

    def cut(x, block):
        return cmap(lambda v: v[:, block * LANES : (block + 1) * LANES], x)

    coefs = [coefficient(depth_line, wide(own, START, row)) for row in range(out_rows)]
    forces = [(wide(own, RE, row), wide(own, IM, row)) for row in range(out_rows)]
    medium = segment_medium(depth_line, coefs)
    source = segment_source(depth_line, coefs, forces, medium[0], medium[2])
    mediums = [tuple(cut(v, block) for v in medium) for block in range(nx)]
    sources = [tuple(cut(v, block) for v in source) for block in range(nx)]
    total_medium, levels = medium_list(mediums)
    total_source, inners = source_list(levels, sources)
    for row, part in enumerate(v for pair in (*total_medium, *total_source) for v in pair):
        summary[pl.ds(row, slots, stride=SUMMARY_ROWS), :] = part

    def sum_copy(tile, origin):
        return pltpu.make_async_remote_copy(
            src_ref=summary.at[pl.ds(tile * SUMMARY_ROWS, SUMMARY_ROWS), :],
            dst_ref=gathered.at[pl.ds(pl.multiple_of(origin * SUMMARY_ROWS, SUMMARY_ROWS), SUMMARY_ROWS), :],
            send_sem=sum_send.at[tile],
            recv_sem=sum_recv.at[origin],
            device_id=(tile, xr),
            device_id_type=MESH,
        )

    for tile in range(tiles):

        @pl.when(dep != tile)
        def _():
            sum_copy(tile, dep).start()

    def ans_copy(peer, tile):
        return pltpu.make_async_remote_copy(
            src_ref=answer.at[pl.ds(pl.multiple_of(peer * SUBLANES, SUBLANES), SUBLANES), :],
            dst_ref=boundary.at[pl.ds(pl.multiple_of(tile * SUBLANES, SUBLANES), SUBLANES), :],
            send_sem=ans_send.at[peer],
            recv_sem=ans_recv.at[tile],
            device_id=(peer, xr),
            device_id_type=MESH,
        )

    if tiles < slots:
        boundary[tiles * SUBLANES :, :] = jnp.zeros(((slots - tiles) * SUBLANES, LANES), jnp.float32)

    @pl.when(dep < tiles)
    def _():
        gathered[pl.ds(pl.multiple_of(dep * SUMMARY_ROWS, SUMMARY_ROWS), SUMMARY_ROWS), :] = summary[
            pl.ds(pl.multiple_of(dep * SUMMARY_ROWS, SUMMARY_ROWS), SUMMARY_ROWS), :
        ]
        for offset in range(1, nd):
            sum_copy(0, lax.rem(dep + offset, nd)).wait_recv()
        values = [gathered[pl.ds(row, nd, stride=SUMMARY_ROWS), :] for row in range(10)]
        pairs = [(values[2 * i], values[2 * i + 1]) for i in range(5)]
        all_medium, all_levels = medium_tree(tuple(pairs[:3]), 0, nd)
        all_source, all_inners = source_tree(all_levels, tuple(pairs[3:]), 0)
        p_all, q_all = between_walls(depth_line, all_medium, all_source)
        p_all, q_all = down_tree(all_levels, all_inners, p_all, q_all, 0)
        for row, value in enumerate((*p_all, *q_all)):
            answer[pl.ds(row, nd, stride=SUBLANES), :] = value
        boundary[pl.ds(pl.multiple_of(dep * SUBLANES, SUBLANES), SUBLANES), :] = answer[pl.ds(pl.multiple_of(dep * SUBLANES, SUBLANES), SUBLANES), :]
        for offset in range(1, nd):
            ans_copy(lax.rem(dep + offset, nd), dep).start()

    for offset in range(nx):
        block = peer_at(offset)
        if offset > 0:
            bulk_copy(xr, block, END).wait_recv()
        tall_end[pl.ds(pl.multiple_of(block * LANES, LANES), LANES), :] = received[pl.ds(at(block, END), LANES), :].T
    cross_cells = LANES // SUBLANES

    def tall_strided(ref, *lead):
        return [
            jnp.concatenate(
                [
                    ref[lead + (pl.ds(block * LANES + cell, SUBLANES, stride=cross_cells), slice(None))]
                    for block in range(nx)
                ],
                axis=1,
            )
            for cell in range(cross_cells)
        ]

    def cross_coefs():
        return [coefficient(cross_line, v) for v in tall_strided(tall_end)]

    cross_medium = segment_medium(cross_line, cross_coefs())
    block_medium, block_levels = medium_tree(cross_medium, 0, SUBLANES)
    sub_place = lax.broadcasted_iota(jnp.int32, (SUBLANES, LANES), 0)
    lane_place = lax.broadcasted_iota(jnp.int32, (SUBLANES, LANES), 1)
    used = lane_place < tiles * out_rows

    def packed(value, fill):
        total = jnp.zeros((SUBLANES, LANES), jnp.float32)
        for block in range(nx):
            row = jnp.broadcast_to(value[0:1, block * LANES : (block + 1) * LANES], (SUBLANES, LANES))
            total = jnp.where(sub_place == block, row, total)
        return jnp.where(used, total, fill)

    def unpacked(value):
        return jnp.concatenate(
            [jnp.broadcast_to(value[block : block + 1, :], (SUBLANES, LANES)) for block in range(nx)], axis=1
        )

    packed_medium = tuple(
        (packed(v[0], fill), packed(v[1], 0.0)) for v, fill in zip(block_medium, (1.0, 0.0, 0.0))
    )
    tile_medium, tile_levels = medium_tree(packed_medium, 1, slots, out_rows)
    line_medium, line_levels = medium_tree(tile_medium, 0, nx)

    for tile in range(tiles):

        @pl.when(dep != tile)
        def _():
            ans_copy(dep, tile).wait_recv()

    edge_rows = 4 * slots
    incoming = [boundary[pl.ds(row, slots, stride=SUBLANES), :] for row in range(4)]
    waves = down_list(levels, inners, (incoming[0], incoming[1]), (incoming[2], incoming[3]))
    for block, (p_left, q_right) in enumerate(waves):
        before, here = segment_start(depth_line, mediums[block], sources[block], p_left, q_right)
        for row, value in enumerate((*before, *here)):
            first = block * edge_rows + row * slots
            edge_out[first : first + slots, :] = value

    def edge_at(block):
        return pl.ds(pl.multiple_of(block * edge_rows, edge_rows), edge_rows)

    def edge_copy(peer, source_block):
        return pltpu.make_async_remote_copy(
            src_ref=edge_out.at[edge_at(peer), :],
            dst_ref=edge_in.at[edge_at(source_block), :],
            send_sem=edge_send.at[peer],
            recv_sem=edge_recv.at[source_block],
            device_id=(dep, peer),
            device_id_type=MESH,
        )

    for offset in far_first:
        edge_copy(peer_at(offset), xr).start()
    edge_in[edge_at(xr), :] = edge_out[edge_at(xr), :]

    for group in range(0, nx, 2):
        blocks = [peer_at(group), peer_at(group + 1)]
        for offset, block in enumerate(blocks, group):
            if offset > 0:
                for part in (START, RE, IM):
                    bulk_copy(xr, block, part).wait_recv()
                edge_copy(xr, block).wait_recv()

        def side(ref, first, **keywords):
            return jnp.concatenate([ref[pl.ds(first(block), slots, **keywords), :] for block in blocks], axis=1)

        def row_of(part, row):
            return side(received, lambda block: at(block, part) + row, stride=out_rows)

        def edge_of(row):
            return side(edge_in, lambda block: pl.multiple_of(block * edge_rows + row * slots, SUBLANES))

        before, here = (edge_of(0), edge_of(1)), (edge_of(2), edge_of(3))
        for row in range(out_rows):
            force = (row_of(RE, row), row_of(IM, row))
            value = result(depth_line, force, here)
            for c in range(2):
                for side_at in range(2):
                    place = pl.ds((side_at * 2 + c) * LANES + row, slots, stride=out_rows)
                    middle[place, :] = value[c][:, side_at * LANES : (side_at + 1) * LANES]
            if row < out_rows - 1:
                coef = coefficient(depth_line, row_of(START, row))
                before, here = here, step(depth_line, coef, here, before, force)
        for side_at, block in enumerate(blocks):
            for c in range(2):
                first = (side_at * 2 + c) * LANES
                tall_field[c, pl.ds(pl.multiple_of(block * LANES, LANES), LANES), :] = middle[first : first + LANES, :].T

    coefs = cross_coefs()
    forces = list(zip(tall_strided(tall_field, 0), tall_strided(tall_field, 1)))
    source = segment_source(cross_line, coefs, forces, cross_medium[0], cross_medium[2])
    block_source, block_inners = source_tree(block_levels, source, 0)
    packed_source = tuple((packed(v[0], 0.0), packed(v[1], 0.0)) for v in block_source)
    tile_source, tile_inners = source_tree(tile_levels, packed_source, 1)
    line_source, line_inners = source_tree(line_levels, tile_source, 0)
    p_left, q_right = between_walls(cross_line, line_medium, line_source)
    p_left, q_right = down_tree(line_levels, line_inners, p_left, q_right, 0)
    p_left, q_right = down_tree(tile_levels, tile_inners, p_left, q_right, 1)
    p_left, q_right = cmap(unpacked, p_left), cmap(unpacked, q_right)
    p_left, q_right = down_tree(block_levels, block_inners, p_left, q_right, 0)
    all_before, all_here = segment_start(cross_line, cross_medium, source, p_left, q_right)
    for block in range(nx):
        before, here = cut(all_before, block), cut(all_here, block)
        for cell in range(cross_cells):
            place = pl.ds(block * LANES + cell, SUBLANES, stride=cross_cells)
            force = (tall_field[0, place, :], tall_field[1, place, :])
            value = result(cross_line, force, here)
            tall_out[0, place, :] = value[0]
            tall_out[1, place, :] = value[1]
            if cell < cross_cells - 1:
                coef = coefficient(cross_line, tall_end[place, :])
                before, here = here, step(cross_line, coef, here, before, force)
        for c in range(2):
            flat = tall_out[c, block * LANES : (block + 1) * LANES, :].T
            for tile in range(tiles):
                first = block * width + tile * LANES
                out[c, :, first : first + LANES] = flat[tile * out_rows : (tile + 1) * out_rows, :]

    for offset in range(1, nx):
        peer = peer_at(offset)
        edge_copy(peer, xr).wait_send()
        for part in range(4):
            bulk_copy(peer, xr, part).wait_send()
    for tile in range(tiles):

        @pl.when(dep != tile)
        def _():
            sum_copy(tile, dep).wait_send()

    @pl.when(dep < tiles)
    def _():
        for offset in range(1, nd):
            ans_copy(lax.rem(dep + offset, nd), dep).wait_send()


def local(nd, nx, sound_field, index_start, index_end):
    rows, width = index_start.shape
    tiles = width // LANES
    out_rows = rows // nx
    slots = LANES // out_rows
    assert tiles <= nd and tiles <= slots and slots == SUBLANES and nx <= SUBLANES and nx % 2 == 0

    def blocked(array):
        lead = array.shape[:-2]
        pieces = array.reshape(lead + (nx, out_rows, tiles, LANES))
        pieces = jnp.moveaxis(jnp.swapaxes(pieces, -3, -2), len(lead), 0)
        return pieces.reshape((nx,) + lead + (tiles * out_rows, LANES))

    f32 = jnp.float32
    dma = pltpu.SemaphoreType.DMA
    return pl.pallas_call(
        functools.partial(kernel, nd, nx),
        out_shape=jax.ShapeDtypeStruct((2, out_rows, width * nx), f32),
        in_specs=[pl.BlockSpec(memory_space=pltpu.VMEM)] * 3,
        out_specs=pl.BlockSpec(memory_space=pltpu.VMEM),
        scratch_shapes=[
            pltpu.VMEM((nx * 4 * LANES, LANES), f32),
            pltpu.VMEM((nx * 4 * LANES, LANES), f32),
            pltpu.VMEM((slots * SUMMARY_ROWS, LANES), f32),
            pltpu.VMEM((nd * SUMMARY_ROWS, LANES), f32),
            pltpu.VMEM((nd * SUBLANES, LANES), f32),
            pltpu.VMEM((slots * SUBLANES, LANES), f32),
            pltpu.VMEM((nx * 4 * slots, LANES), f32),
            pltpu.VMEM((nx * 4 * slots, LANES), f32),
            pltpu.VMEM((4 * LANES, LANES), f32),
            pltpu.VMEM((nx * LANES, LANES), f32),
            pltpu.VMEM((2, nx * LANES, LANES), f32),
            pltpu.VMEM((2, nx * LANES, LANES), f32),
            dma((tiles,)),
            dma((nd,)),
            dma((nd,)),
            dma((tiles,)),
            dma((nx, 4)),
            dma((nx, 4)),
            dma((nx,)),
            dma((nx,)),
        ],
        compiler_params=pltpu.CompilerParams(
            collective_id=0, has_side_effects=True, vmem_limit_bytes=32 * 1024 * 1024
        ),
        cost_estimate=pl.CostEstimate(flops=20_000_000, bytes_accessed=2_000_000, transcendentals=0),
    )(blocked(sound_field), blocked(index_start), blocked(index_end))


def solution(mesh):
    nd, nx = mesh.shape["depth"], mesh.shape["xr"]
    in_specs = (P(None, "depth", "xr"), P("depth", "xr"), P("depth", "xr"))
    out_specs = P(None, ("depth", "xr"), None)
    return jax.shard_map(
        functools.partial(local, nd, nx), mesh=mesh, in_specs=in_specs, out_specs=out_specs, check_vma=False
    )
```

```python
import functools

import jax
import jax.numpy as jnp
from jax import lax
from jax.experimental import pallas as pl
from jax.experimental.pallas import tpu as pltpu
from jax.sharding import PartitionSpec as P
import numpy as np

depth_stiffness = 1.6
cross_stiffness = 1.2
numer = 2.857 + 0.004j
denom = 2.857 - 0.004j
LANES = 128
SUBLANES = 8
SUMMARY_ROWS = 16
MESH = pl.DeviceIdType.MESH


class Line:
    def __init__(self, stiffness):
        shift = 1.0 / denom
        self.slope = -0.5 / stiffness
        self.level = 2.0 - shift.real / stiffness + 0.5 / stiffness
        self.damping = shift.imag / stiffness
        cosine = 0.5 * (self.level + self.slope * 0.89)
        angle = float(np.arccos(cosine))
        self.mu = complex(np.exp(0.5j * angle))
        self.nu = self.mu.conjugate()
        self.inv_det = 1.0 / (self.nu * self.nu - self.mu * self.mu)
        self.wall = -self.mu * self.mu
        self.alpha = numer / denom
        self.beta = (denom - numer) / (denom * denom * stiffness)


def mul(x, y):
    return (x[0] * y[0] - x[1] * y[1], x[0] * y[1] + x[1] * y[0])


def add(x, y):
    return (x[0] + y[0], x[1] + y[1])


def sub(x, y):
    return (x[0] - y[0], x[1] - y[1])


def cmul(c, x):
    c = complex(c)
    return (c.real * x[0] - c.imag * x[1], c.real * x[1] + c.imag * x[0])


def recip(x):
    scale = 1.0 / (x[0] * x[0] + x[1] * x[1])
    return (x[0] * scale, -x[1] * scale)


def one_minus(x):
    return (1.0 - x[0], -x[1])


def cmap(fn, x):
    return (fn(x[0]), fn(x[1]))


def step(line, coef, here, before, force=None):
    real = coef * here[0] + line.damping * here[1] - before[0]
    imag = coef * here[1] - line.damping * here[0] - before[1]
    if force is not None:
        real, imag = real + force[0], imag + force[1]
    return (real, imag)


def coefficient(line, index):
    return line.level + line.slope * index


def segment_medium(line, coefs):
    shape = coefs[0].shape
    def const(c):
        return (jnp.full(shape, c.real, jnp.float32), jnp.full(shape, c.imag, jnp.float32))
    p0, p1 = const(line.nu), const(line.mu)
    q0, q1 = const(line.mu), const(line.nu)
    for coef in coefs:
        p0, p1 = p1, step(line, coef, p1, p0)
        q0, q1 = q1, step(line, coef, q1, q0)
    lower, upper = -line.mu * line.inv_det, line.nu * line.inv_det
    t21 = add(cmul(lower, p0), cmul(upper, p1))
    t22 = add(cmul(lower, q0), cmul(upper, q1))
    t12 = add(cmul(upper, q0), cmul(lower, q1))
    t = recip(t22)
    r1 = mul(t21, t)
    r1 = (-r1[0], -r1[1])
    r2 = mul(t12, t)
    return t, r1, r2


def segment_source(line, coefs, forces, t, r2):
    zero = jnp.zeros(coefs[0].shape, jnp.float32)
    v0, v1 = (zero, zero), (zero, zero)
    for position, (coef, force) in enumerate(zip(coefs, forces)):
        if position == 0:
            v0, v1 = v1, force
        else:
            v0, v1 = v1, step(line, coef, v1, v0, force)
    lower, upper = -line.mu * line.inv_det, line.nu * line.inv_det
    right = add(cmul(upper, v0), cmul(lower, v1))
    left = add(cmul(lower, v0), cmul(upper, v1))
    s1 = mul(left, t)
    s1 = (-s1[0], -s1[1])
    s2 = sub(right, mul(r2, left))
    return s1, s2


def from_right(x, axis, amount):
    return cmap(lambda v: pltpu.roll(v, v.shape[axis] - amount, axis), x)


def from_left(x, axis, amount):
    return cmap(lambda v: pltpu.roll(v, amount, axis), x)


def merge_medium(left, right):
    t_a, r1_a, r2_a = left
    t_b, r1_b, r2_b = right
    d = recip(one_minus(mul(r2_a, r1_b)))
    ra, rb = mul(d, r2_a), mul(d, r1_b)
    tad, tbd = mul(t_a, d), mul(t_b, d)
    x1, x2 = mul(t_a, rb), mul(t_b, ra)
    merged = (mul(tad, t_b), add(r1_a, mul(x1, t_a)), add(r2_b, mul(x2, t_b)))
    return merged, (d, ra, rb, t_a, t_b, tad, tbd, x1, x2)


def merge_source(kept, left, right):
    d, ra, rb, t_a, t_b, tad, tbd, x1, x2 = kept
    s1_a, s2_a = left
    s1_b, s2_b = right
    e_p = add(mul(d, s2_a), mul(ra, s1_b))
    e_q = add(mul(d, s1_b), mul(rb, s2_a))
    merged = (add(s1_a, mul(t_a, e_q)), add(s2_b, mul(t_b, e_p)))
    return merged, (e_p, e_q)


def middle_waves(kept, inner, p_left, q_right):
    d, ra, rb, t_a, t_b, tad, tbd, x1, x2 = kept
    p_mid = add(add(mul(tad, p_left), mul(x2, q_right)), inner[0])
    q_mid = add(add(mul(x1, p_left), mul(tbd, q_right)), inner[1])
    return p_mid, q_mid


def medium_list(items):
    levels = []
    while len(items) > 1:
        pairs = [merge_medium(a, b) for a, b in zip(items[0::2], items[1::2])]
        items = [merged for merged, _ in pairs]
        levels.append([kept for _, kept in pairs])
    return items[0], levels


def source_list(levels, items):
    inners = []
    for level in levels:
        pairs = [merge_source(kept, a, b) for kept, a, b in zip(level, items[0::2], items[1::2])]
        items = [merged for merged, _ in pairs]
        inners.append([inner for _, inner in pairs])
    return items[0], inners


def down_list(levels, inners, p_left, q_right):
    waves = [(p_left, q_right)]
    for level, inner_level in zip(reversed(levels), reversed(inners)):
        finer = []
        for kept, inner, (p, q) in zip(level, inner_level, waves):
            p_mid, q_mid = middle_waves(kept, inner, p, q)
            finer += [(p, q_mid), (p_mid, q)]
        waves = finer
    return waves


def medium_level(medium, axis, amount):
    return merge_medium(medium, tuple(from_right(v, axis, amount) for v in medium))


def source_level(kept, source, axis, amount):
    return merge_source(kept, source, tuple(from_right(v, axis, amount) for v in source))


def down_level(kept, inner, p_left, q_right, axis, amount):
    p_mid, q_mid = middle_waves(kept, inner, p_left, q_right)
    shape = p_left[0].shape
    place = lax.broadcasted_iota(jnp.int32, shape, axis)
    is_left = (place % (2 * amount)) < amount
    p_moved = from_left(p_mid, axis, amount)
    q_moved = from_left(q_right, axis, amount)
    p_new = tuple(jnp.where(is_left, a, b) for a, b in zip(p_left, p_moved))
    q_new = tuple(jnp.where(is_left, a, b) for a, b in zip(q_mid, q_moved))
    return p_new, q_new


def medium_tree(medium, axis, count, unit=1):
    levels = []
    amount = unit
    while amount < count * unit:
        medium, kept = medium_level(medium, axis, amount)
        levels.append((amount, kept))
        amount *= 2
    return medium, levels


def source_tree(levels, source, axis):
    inners = []
    for amount, kept in levels:
        source, inner = source_level(kept, source, axis, amount)
        inners.append(inner)
    return source, inners


def down_tree(levels, inners, p_left, q_right, axis):
    for (amount, kept), inner in zip(reversed(levels), reversed(inners)):
        p_left, q_right = down_level(kept, inner, p_left, q_right, axis, amount)
    return p_left, q_right


def between_walls(line, medium, source):
    t, r1, r2 = medium
    s1, s2 = source
    tw = cmul(line.wall, t)
    first = one_minus(cmul(line.wall, r1))
    second = one_minus(cmul(line.wall, r2))
    scale = recip(sub(mul(first, second), mul(tw, tw)))
    q_left = mul(scale, add(mul(second, s1), mul(tw, s2)))
    p_right = mul(scale, add(mul(tw, s1), mul(first, s2)))
    return cmul(line.wall, q_left), cmul(line.wall, p_right)


def segment_start(line, medium, source, p_left, q_right):
    t, r1, r2 = medium
    q_left = add(add(mul(r1, p_left), mul(t, q_right)), source[0])
    before = add(cmul(line.nu, p_left), cmul(line.mu, q_left))
    here = add(cmul(line.mu, p_left), cmul(line.nu, q_left))
    return before, here


def result(line, force, here):
    return add(cmul(line.alpha, force), cmul(line.beta, here))


def kernel(
    nd, nx, field_in, start_in, end_in, out,
    field, start, end, own, received, summary, gathered, answer, boundary, edge_out, edge_in,
    middle, tall_end, tall_field, tall_out,
    sum_send, sum_recv, ans_send, ans_recv, bulk_send, bulk_recv, edge_send, edge_recv, load_sem,
):
    width = out.shape[2] // nx
    tiles = width // LANES
    out_rows = out.shape[1]
    used_rows = tiles * out_rows
    loads = [
        pltpu.make_async_copy(source_ref, dest_ref, load_sem.at[which])
        for which, (source_ref, dest_ref) in enumerate(((end_in, end), (start_in, start), (field_in, field)))
    ]
    for load in loads:
        load.start()
    slots = LANES // out_rows
    dep = lax.axis_index("depth")
    xr = lax.axis_index("xr")
    depth_line = Line(depth_stiffness)
    cross_line = Line(cross_stiffness)

    barrier = pltpu.get_barrier_semaphore()

    @pl.loop(1, nd)
    def _(offset):
        pl.semaphore_signal(barrier, 1, device_id=(lax.rem(dep + offset, nd), xr), device_id_type=MESH)

    @pl.loop(1, nx)
    def _(offset):
        pl.semaphore_signal(barrier, 1, device_id=(dep, lax.rem(xr + offset, nx)), device_id_type=MESH)

    def peer_at(offset):
        base = xr // 2 * 2
        return lax.rem(base + 2 * (offset // 2), nx) + lax.rem(xr + offset, 2)

    RE, IM, START, END = range(4)

    def at(block, part):
        return pl.multiple_of((block * 4 + part) * LANES, LANES)

    def bulk_copy(peer, source_block, part):
        return pltpu.make_async_remote_copy(
            src_ref=own.at[pl.ds(at(peer, part), used_rows), :],
            dst_ref=received.at[pl.ds(at(source_block, part), used_rows), :],
            send_sem=bulk_send.at[peer, part],
            recv_sem=bulk_recv.at[source_block, part],
            device_id=(dep, peer),
            device_id_type=MESH,
        )

    far_first = list(range(2, nx)) + [1]

    def block_own(part):
        for block in range(nx):
            base = (block * 4 + part) * LANES
            for tile in range(tiles):
                place = (slice(block * out_rows, (block + 1) * out_rows), slice(tile * LANES, (tile + 1) * LANES))
                piece = field[(part,) + place] if part < 2 else (start if part == START else end)[place]
                own[base + tile * out_rows : base + (tile + 1) * out_rows, :] = piece

    for load, parts in zip(loads, ((END,), (START,), (RE, IM))):
        load.wait()
        for part in parts:
            block_own(part)
    pl.semaphore_wait(barrier, nd - 1 + nx - 1)
    for part in (END, START, RE, IM):
        for offset in far_first:
            bulk_copy(peer_at(offset), xr, part).start()

    if used_rows < LANES:
        for block in range(nx):
            for part in range(4):
                base = (block * 4 + part) * LANES
                pad = jnp.full((LANES - used_rows, LANES), 0.0 if part < 2 else 0.89, jnp.float32)
                received[base + used_rows : base + LANES, :] = pad
                own[base + used_rows : base + LANES, :] = pad
    for part in range(4):
        received[pl.ds(at(xr, part), used_rows), :] = own[pl.ds(at(xr, part), used_rows), :]

    def wide(ref, part, row):
        return jnp.concatenate(
            [ref[pl.ds((block * 4 + part) * LANES + row, slots, stride=out_rows), :] for block in range(nx)], axis=1
        )

    def cut(x, block):
        return cmap(lambda v: v[:, block * LANES : (block + 1) * LANES], x)

    coefs = [coefficient(depth_line, wide(own, START, row)) for row in range(out_rows)]
    forces = [(wide(own, RE, row), wide(own, IM, row)) for row in range(out_rows)]
    medium = segment_medium(depth_line, coefs)
    source = segment_source(depth_line, coefs, forces, medium[0], medium[2])
    mediums = [tuple(cut(v, block) for v in medium) for block in range(nx)]
    sources = [tuple(cut(v, block) for v in source) for block in range(nx)]
    total_medium, levels = medium_list(mediums)
    total_source, inners = source_list(levels, sources)
    for row, part in enumerate(v for pair in (*total_medium, *total_source) for v in pair):
        summary[pl.ds(row, slots, stride=SUMMARY_ROWS), :] = part

    def sum_copy(tile, origin):
        return pltpu.make_async_remote_copy(
            src_ref=summary.at[pl.ds(tile * SUMMARY_ROWS, SUMMARY_ROWS), :],
            dst_ref=gathered.at[pl.ds(pl.multiple_of(origin * SUMMARY_ROWS, SUMMARY_ROWS), SUMMARY_ROWS), :],
            send_sem=sum_send.at[tile],
            recv_sem=sum_recv.at[origin],
            device_id=(tile, xr),
            device_id_type=MESH,
        )

    for tile in range(tiles):

        @pl.when(dep != tile)
        def _():
            sum_copy(tile, dep).start()

    def ans_copy(peer, tile):
        return pltpu.make_async_remote_copy(
            src_ref=answer.at[pl.ds(pl.multiple_of(peer * SUBLANES, SUBLANES), SUBLANES), :],
            dst_ref=boundary.at[pl.ds(pl.multiple_of(tile * SUBLANES, SUBLANES), SUBLANES), :],
            send_sem=ans_send.at[peer],
            recv_sem=ans_recv.at[tile],
            device_id=(peer, xr),
            device_id_type=MESH,
        )

    if tiles < slots:
        boundary[tiles * SUBLANES :, :] = jnp.zeros(((slots - tiles) * SUBLANES, LANES), jnp.float32)

    @pl.when(dep < tiles)
    def _():
        gathered[pl.ds(pl.multiple_of(dep * SUMMARY_ROWS, SUMMARY_ROWS), SUMMARY_ROWS), :] = summary[
            pl.ds(pl.multiple_of(dep * SUMMARY_ROWS, SUMMARY_ROWS), SUMMARY_ROWS), :
        ]
        for offset in range(1, nd):
            sum_copy(0, lax.rem(dep + offset, nd)).wait_recv()
        values = [gathered[pl.ds(row, nd, stride=SUMMARY_ROWS), :] for row in range(10)]
        pairs = [(values[2 * i], values[2 * i + 1]) for i in range(5)]
        all_medium, all_levels = medium_tree(tuple(pairs[:3]), 0, nd)
        all_source, all_inners = source_tree(all_levels, tuple(pairs[3:]), 0)
        p_all, q_all = between_walls(depth_line, all_medium, all_source)
        p_all, q_all = down_tree(all_levels, all_inners, p_all, q_all, 0)
        for row, value in enumerate((*p_all, *q_all)):
            answer[pl.ds(row, nd, stride=SUBLANES), :] = value
        boundary[pl.ds(pl.multiple_of(dep * SUBLANES, SUBLANES), SUBLANES), :] = answer[pl.ds(pl.multiple_of(dep * SUBLANES, SUBLANES), SUBLANES), :]
        for offset in range(1, nd):
            ans_copy(lax.rem(dep + offset, nd), dep).start()

    for offset in range(nx):
        block = peer_at(offset)
        if offset > 0:
            bulk_copy(xr, block, END).wait_recv()
        tall_end[pl.ds(pl.multiple_of(block * LANES, LANES), LANES), :] = received[pl.ds(at(block, END), LANES), :].T
    cross_cells = LANES // SUBLANES

    def tall_strided(ref, *lead):
        return [
            jnp.concatenate(
                [
                    ref[lead + (pl.ds(block * LANES + cell, SUBLANES, stride=cross_cells), slice(None))]
                    for block in range(nx)
                ],
                axis=1,
            )
            for cell in range(cross_cells)
        ]

    def cross_coefs():
        return [coefficient(cross_line, v) for v in tall_strided(tall_end)]

    cross_medium = segment_medium(cross_line, cross_coefs())
    block_medium, block_levels = medium_tree(cross_medium, 0, SUBLANES)
    sub_place = lax.broadcasted_iota(jnp.int32, (SUBLANES, LANES), 0)
    lane_place = lax.broadcasted_iota(jnp.int32, (SUBLANES, LANES), 1)
    used = lane_place < tiles * out_rows

    def packed(value, fill):
        total = jnp.zeros((SUBLANES, LANES), jnp.float32)
        for block in range(nx):
            row = jnp.broadcast_to(value[0:1, block * LANES : (block + 1) * LANES], (SUBLANES, LANES))
            total = jnp.where(sub_place == block, row, total)
        return jnp.where(used, total, fill)

    def unpacked(value):
        return jnp.concatenate(
            [jnp.broadcast_to(value[block : block + 1, :], (SUBLANES, LANES)) for block in range(nx)], axis=1
        )

    packed_medium = tuple(
        (packed(v[0], fill), packed(v[1], 0.0)) for v, fill in zip(block_medium, (1.0, 0.0, 0.0))
    )
    tile_medium, tile_levels = medium_tree(packed_medium, 1, slots, out_rows)
    line_medium, line_levels = medium_tree(tile_medium, 0, nx)

    for tile in range(tiles):

        @pl.when(dep != tile)
        def _():
            ans_copy(dep, tile).wait_recv()

    edge_rows = 4 * slots
    incoming = [boundary[pl.ds(row, slots, stride=SUBLANES), :] for row in range(4)]
    waves = down_list(levels, inners, (incoming[0], incoming[1]), (incoming[2], incoming[3]))
    for block, (p_left, q_right) in enumerate(waves):
        before, here = segment_start(depth_line, mediums[block], sources[block], p_left, q_right)
        for row, value in enumerate((*before, *here)):
            first = block * edge_rows + row * slots
            edge_out[first : first + slots, :] = value

    def edge_at(block):
        return pl.ds(pl.multiple_of(block * edge_rows, edge_rows), edge_rows)

    def edge_copy(peer, source_block):
        return pltpu.make_async_remote_copy(
            src_ref=edge_out.at[edge_at(peer), :],
            dst_ref=edge_in.at[edge_at(source_block), :],
            send_sem=edge_send.at[peer],
            recv_sem=edge_recv.at[source_block],
            device_id=(dep, peer),
            device_id_type=MESH,
        )

    for offset in far_first:
        edge_copy(peer_at(offset), xr).start()
    edge_in[edge_at(xr), :] = edge_out[edge_at(xr), :]

    for group in range(0, nx, 2):
        blocks = [peer_at(group), peer_at(group + 1)]
        for offset, block in enumerate(blocks, group):
            if offset > 0:
                for part in (START, RE, IM):
                    bulk_copy(xr, block, part).wait_recv()
                edge_copy(xr, block).wait_recv()

        def side(ref, first, **keywords):
            return jnp.concatenate([ref[pl.ds(first(block), slots, **keywords), :] for block in blocks], axis=1)

        def row_of(part, row):
            return side(received, lambda block: at(block, part) + row, stride=out_rows)

        def edge_of(row):
            return side(edge_in, lambda block: pl.multiple_of(block * edge_rows + row * slots, SUBLANES))

        before, here = (edge_of(0), edge_of(1)), (edge_of(2), edge_of(3))
        for row in range(out_rows):
            force = (row_of(RE, row), row_of(IM, row))
            value = result(depth_line, force, here)
            for c in range(2):
                for side_at in range(2):
                    place = pl.ds((side_at * 2 + c) * LANES + row, slots, stride=out_rows)
                    middle[place, :] = value[c][:, side_at * LANES : (side_at + 1) * LANES]
            if row < out_rows - 1:
                coef = coefficient(depth_line, row_of(START, row))
                before, here = here, step(depth_line, coef, here, before, force)
        for side_at, block in enumerate(blocks):
            for c in range(2):
                first = (side_at * 2 + c) * LANES
                tall_field[c, pl.ds(pl.multiple_of(block * LANES, LANES), LANES), :] = middle[first : first + LANES, :].T

    coefs = cross_coefs()
    forces = list(zip(tall_strided(tall_field, 0), tall_strided(tall_field, 1)))
    source = segment_source(cross_line, coefs, forces, cross_medium[0], cross_medium[2])
    block_source, block_inners = source_tree(block_levels, source, 0)
    packed_source = tuple((packed(v[0], 0.0), packed(v[1], 0.0)) for v in block_source)
    tile_source, tile_inners = source_tree(tile_levels, packed_source, 1)
    line_source, line_inners = source_tree(line_levels, tile_source, 0)
    p_left, q_right = between_walls(cross_line, line_medium, line_source)
    p_left, q_right = down_tree(line_levels, line_inners, p_left, q_right, 0)
    p_left, q_right = down_tree(tile_levels, tile_inners, p_left, q_right, 1)
    p_left, q_right = cmap(unpacked, p_left), cmap(unpacked, q_right)
    p_left, q_right = down_tree(block_levels, block_inners, p_left, q_right, 0)
    all_before, all_here = segment_start(cross_line, cross_medium, source, p_left, q_right)
    for block in range(nx):
        before, here = cut(all_before, block), cut(all_here, block)
        for cell in range(cross_cells):
            place = pl.ds(block * LANES + cell, SUBLANES, stride=cross_cells)
            force = (tall_field[0, place, :], tall_field[1, place, :])
            value = result(cross_line, force, here)
            tall_out[0, place, :] = value[0]
            tall_out[1, place, :] = value[1]
            if cell < cross_cells - 1:
                coef = coefficient(cross_line, tall_end[place, :])
                before, here = here, step(cross_line, coef, here, before, force)
        for c in range(2):
            flat = tall_out[c, block * LANES : (block + 1) * LANES, :].T
            for tile in range(tiles):
                first = block * width + tile * LANES
                out[c, :, first : first + LANES] = flat[tile * out_rows : (tile + 1) * out_rows, :]

    for offset in range(1, nx):
        peer = peer_at(offset)
        edge_copy(peer, xr).wait_send()
        for part in range(4):
            bulk_copy(peer, xr, part).wait_send()
    for tile in range(tiles):

        @pl.when(dep != tile)
        def _():
            sum_copy(tile, dep).wait_send()

    @pl.when(dep < tiles)
    def _():
        for offset in range(1, nd):
            ans_copy(lax.rem(dep + offset, nd), dep).wait_send()


def local(nd, nx, sound_field, index_start, index_end):
    rows, width = index_start.shape
    tiles = width // LANES
    out_rows = rows // nx
    slots = LANES // out_rows
    assert tiles <= nd and tiles <= slots and slots == SUBLANES and nx <= SUBLANES and nx % 2 == 0

    f32 = jnp.float32
    dma = pltpu.SemaphoreType.DMA
    return pl.pallas_call(
        functools.partial(kernel, nd, nx),
        out_shape=jax.ShapeDtypeStruct((2, out_rows, width * nx), f32),
        in_specs=[pl.BlockSpec(memory_space=pltpu.HBM)] * 3,
        out_specs=pl.BlockSpec(memory_space=pltpu.VMEM),
        scratch_shapes=[
            pltpu.VMEM((2, rows, width), f32),
            pltpu.VMEM((rows, width), f32),
            pltpu.VMEM((rows, width), f32),
            pltpu.VMEM((nx * 4 * LANES, LANES), f32),
            pltpu.VMEM((nx * 4 * LANES, LANES), f32),
            pltpu.VMEM((slots * SUMMARY_ROWS, LANES), f32),
            pltpu.VMEM((nd * SUMMARY_ROWS, LANES), f32),
            pltpu.VMEM((nd * SUBLANES, LANES), f32),
            pltpu.VMEM((slots * SUBLANES, LANES), f32),
            pltpu.VMEM((nx * 4 * slots, LANES), f32),
            pltpu.VMEM((nx * 4 * slots, LANES), f32),
            pltpu.VMEM((4 * LANES, LANES), f32),
            pltpu.VMEM((nx * LANES, LANES), f32),
            pltpu.VMEM((2, nx * LANES, LANES), f32),
            pltpu.VMEM((2, nx * LANES, LANES), f32),
            dma((tiles,)),
            dma((nd,)),
            dma((nd,)),
            dma((tiles,)),
            dma((nx, 4)),
            dma((nx, 4)),
            dma((nx,)),
            dma((nx,)),
            dma((3,)),
        ],
        compiler_params=pltpu.CompilerParams(
            collective_id=0, has_side_effects=True, vmem_limit_bytes=64 * 1024 * 1024
        ),
        cost_estimate=pl.CostEstimate(flops=20_000_000, bytes_accessed=2_000_000, transcendentals=0),
    )(sound_field, index_start, index_end)


def solution(mesh):
    nd, nx = mesh.shape["depth"], mesh.shape["xr"]
    in_specs = (P(None, "depth", "xr"), P("depth", "xr"), P("depth", "xr"))
    out_specs = P(None, ("depth", "xr"), None)
    return jax.shard_map(
        functools.partial(local, nd, nx), mesh=mesh, in_specs=in_specs, out_specs=out_specs, check_vma=False
    )
```

```python
import functools

import jax
import jax.numpy as jnp
from jax import lax
from jax.experimental import pallas as pl
from jax.experimental.pallas import tpu as pltpu
from jax.sharding import PartitionSpec as P
import numpy as np

depth_stiffness = 1.6
cross_stiffness = 1.2
numer = 2.857 + 0.004j
denom = 2.857 - 0.004j
LANES = 128
SUBLANES = 8
SUMMARY_ROWS = 16
MESH = pl.DeviceIdType.MESH


class Line:
    def __init__(self, stiffness):
        shift = 1.0 / denom
        self.slope = -0.5 / stiffness
        self.level = 2.0 - shift.real / stiffness + 0.5 / stiffness
        self.damping = shift.imag / stiffness
        cosine = 0.5 * (self.level + self.slope * 0.89)
        angle = float(np.arccos(cosine))
        self.mu = complex(np.exp(0.5j * angle))
        self.nu = self.mu.conjugate()
        self.inv_det = 1.0 / (self.nu * self.nu - self.mu * self.mu)
        self.wall = -self.mu * self.mu
        self.alpha = numer / denom
        self.beta = (denom - numer) / (denom * denom * stiffness)


def mul(x, y):
    return (x[0] * y[0] - x[1] * y[1], x[0] * y[1] + x[1] * y[0])


def add(x, y):
    return (x[0] + y[0], x[1] + y[1])


def sub(x, y):
    return (x[0] - y[0], x[1] - y[1])


def cmul(c, x):
    c = complex(c)
    return (c.real * x[0] - c.imag * x[1], c.real * x[1] + c.imag * x[0])


def recip(x):
    scale = 1.0 / (x[0] * x[0] + x[1] * x[1])
    return (x[0] * scale, -x[1] * scale)


def one_minus(x):
    return (1.0 - x[0], -x[1])


def cmap(fn, x):
    return (fn(x[0]), fn(x[1]))


def step(line, coef, here, before, force=None):
    real = coef * here[0] + line.damping * here[1] - before[0]
    imag = coef * here[1] - line.damping * here[0] - before[1]
    if force is not None:
        real, imag = real + force[0], imag + force[1]
    return (real, imag)


def coefficient(line, index):
    return line.level + line.slope * index


def segment_medium(line, coefs):
    shape = coefs[0].shape
    def const(c):
        return (jnp.full(shape, c.real, jnp.float32), jnp.full(shape, c.imag, jnp.float32))
    p0, p1 = const(line.nu), const(line.mu)
    q0, q1 = const(line.mu), const(line.nu)
    for coef in coefs:
        p0, p1 = p1, step(line, coef, p1, p0)
        q0, q1 = q1, step(line, coef, q1, q0)
    lower, upper = -line.mu * line.inv_det, line.nu * line.inv_det
    t21 = add(cmul(lower, p0), cmul(upper, p1))
    t22 = add(cmul(lower, q0), cmul(upper, q1))
    t12 = add(cmul(upper, q0), cmul(lower, q1))
    t = recip(t22)
    r1 = mul(t21, t)
    r1 = (-r1[0], -r1[1])
    r2 = mul(t12, t)
    return t, r1, r2


def segment_source(line, coefs, forces, t, r2):
    zero = jnp.zeros(coefs[0].shape, jnp.float32)
    v0, v1 = (zero, zero), (zero, zero)
    for position, (coef, force) in enumerate(zip(coefs, forces)):
        if position == 0:
            v0, v1 = v1, force
        else:
            v0, v1 = v1, step(line, coef, v1, v0, force)
    lower, upper = -line.mu * line.inv_det, line.nu * line.inv_det
    right = add(cmul(upper, v0), cmul(lower, v1))
    left = add(cmul(lower, v0), cmul(upper, v1))
    s1 = mul(left, t)
    s1 = (-s1[0], -s1[1])
    s2 = sub(right, mul(r2, left))
    return s1, s2


def from_right(x, axis, amount):
    return cmap(lambda v: pltpu.roll(v, v.shape[axis] - amount, axis), x)


def from_left(x, axis, amount):
    return cmap(lambda v: pltpu.roll(v, amount, axis), x)


def merge_medium(left, right):
    t_a, r1_a, r2_a = left
    t_b, r1_b, r2_b = right
    d = recip(one_minus(mul(r2_a, r1_b)))
    ra, rb = mul(d, r2_a), mul(d, r1_b)
    tad, tbd = mul(t_a, d), mul(t_b, d)
    x1, x2 = mul(t_a, rb), mul(t_b, ra)
    merged = (mul(tad, t_b), add(r1_a, mul(x1, t_a)), add(r2_b, mul(x2, t_b)))
    return merged, (d, ra, rb, t_a, t_b, tad, tbd, x1, x2)


def merge_source(kept, left, right):
    d, ra, rb, t_a, t_b, tad, tbd, x1, x2 = kept
    s1_a, s2_a = left
    s1_b, s2_b = right
    e_p = add(mul(d, s2_a), mul(ra, s1_b))
    e_q = add(mul(d, s1_b), mul(rb, s2_a))
    merged = (add(s1_a, mul(t_a, e_q)), add(s2_b, mul(t_b, e_p)))
    return merged, (e_p, e_q)


def middle_waves(kept, inner, p_left, q_right):
    d, ra, rb, t_a, t_b, tad, tbd, x1, x2 = kept
    p_mid = add(add(mul(tad, p_left), mul(x2, q_right)), inner[0])
    q_mid = add(add(mul(x1, p_left), mul(tbd, q_right)), inner[1])
    return p_mid, q_mid


def medium_list(items):
    levels = []
    while len(items) > 1:
        pairs = [merge_medium(a, b) for a, b in zip(items[0::2], items[1::2])]
        items = [merged for merged, _ in pairs]
        levels.append([kept for _, kept in pairs])
    return items[0], levels


def source_list(levels, items):
    inners = []
    for level in levels:
        pairs = [merge_source(kept, a, b) for kept, a, b in zip(level, items[0::2], items[1::2])]
        items = [merged for merged, _ in pairs]
        inners.append([inner for _, inner in pairs])
    return items[0], inners


def down_list(levels, inners, p_left, q_right):
    waves = [(p_left, q_right)]
    for level, inner_level in zip(reversed(levels), reversed(inners)):
        finer = []
        for kept, inner, (p, q) in zip(level, inner_level, waves):
            p_mid, q_mid = middle_waves(kept, inner, p, q)
            finer += [(p, q_mid), (p_mid, q)]
        waves = finer
    return waves


def medium_level(medium, axis, amount):
    return merge_medium(medium, tuple(from_right(v, axis, amount) for v in medium))


def source_level(kept, source, axis, amount):
    return merge_source(kept, source, tuple(from_right(v, axis, amount) for v in source))


def down_level(kept, inner, p_left, q_right, axis, amount):
    p_mid, q_mid = middle_waves(kept, inner, p_left, q_right)
    shape = p_left[0].shape
    place = lax.broadcasted_iota(jnp.int32, shape, axis)
    is_left = (place % (2 * amount)) < amount
    p_moved = from_left(p_mid, axis, amount)
    q_moved = from_left(q_right, axis, amount)
    p_new = tuple(jnp.where(is_left, a, b) for a, b in zip(p_left, p_moved))
    q_new = tuple(jnp.where(is_left, a, b) for a, b in zip(q_mid, q_moved))
    return p_new, q_new


def medium_tree(medium, axis, count, unit=1):
    levels = []
    amount = unit
    while amount < count * unit:
        medium, kept = medium_level(medium, axis, amount)
        levels.append((amount, kept))
        amount *= 2
    return medium, levels


def source_tree(levels, source, axis):
    inners = []
    for amount, kept in levels:
        source, inner = source_level(kept, source, axis, amount)
        inners.append(inner)
    return source, inners


def down_tree(levels, inners, p_left, q_right, axis):
    for (amount, kept), inner in zip(reversed(levels), reversed(inners)):
        p_left, q_right = down_level(kept, inner, p_left, q_right, axis, amount)
    return p_left, q_right


def between_walls(line, medium, source):
    t, r1, r2 = medium
    s1, s2 = source
    tw = cmul(line.wall, t)
    first = one_minus(cmul(line.wall, r1))
    second = one_minus(cmul(line.wall, r2))
    scale = recip(sub(mul(first, second), mul(tw, tw)))
    q_left = mul(scale, add(mul(second, s1), mul(tw, s2)))
    p_right = mul(scale, add(mul(tw, s1), mul(first, s2)))
    return cmul(line.wall, q_left), cmul(line.wall, p_right)


def segment_start(line, medium, source, p_left, q_right):
    t, r1, r2 = medium
    q_left = add(add(mul(r1, p_left), mul(t, q_right)), source[0])
    before = add(cmul(line.nu, p_left), cmul(line.mu, q_left))
    here = add(cmul(line.mu, p_left), cmul(line.nu, q_left))
    return before, here


def result(line, force, here):
    return add(cmul(line.alpha, force), cmul(line.beta, here))


def kernel(
    nd, nx, field, start, end, out,
    own, received, summary, gathered, answer, boundary, edge_out, edge_in,
    middle, tall_end, tall_field, tall_out,
    sum_send, sum_recv, ans_send, ans_recv, bulk_send, bulk_recv, edge_send, edge_recv,
):
    width = out.shape[2] // nx
    tiles = width // LANES
    out_rows = out.shape[1]
    used_rows = tiles * out_rows
    slots = LANES // out_rows
    dep = lax.axis_index("depth")
    xr = lax.axis_index("xr")
    depth_line = Line(depth_stiffness)
    cross_line = Line(cross_stiffness)

    barrier = pltpu.get_barrier_semaphore()

    @pl.loop(1, nd)
    def _(offset):
        pl.semaphore_signal(barrier, 1, device_id=(lax.rem(dep + offset, nd), xr), device_id_type=MESH)

    @pl.loop(1, nx)
    def _(offset):
        pl.semaphore_signal(barrier, 1, device_id=(dep, lax.rem(xr + offset, nx)), device_id_type=MESH)

    def peer_at(offset):
        base = xr // 2 * 2
        return lax.rem(base + 2 * (offset // 2), nx) + lax.rem(xr + offset, 2)

    RE, IM, START, END = range(4)

    def at(block, part):
        return pl.multiple_of((block * 4 + part) * LANES, LANES)

    def bulk_copy(peer, source_block, part):
        return pltpu.make_async_remote_copy(
            src_ref=own.at[pl.ds(at(peer, part), used_rows), :],
            dst_ref=received.at[pl.ds(at(source_block, part), used_rows), :],
            send_sem=bulk_send.at[peer, part],
            recv_sem=bulk_recv.at[source_block, part],
            device_id=(dep, peer),
            device_id_type=MESH,
        )

    far_first = list(range(2, nx)) + [1]

    def block_own(part):
        for block in range(nx):
            base = (block * 4 + part) * LANES
            for tile in range(tiles):
                place = (slice(block * out_rows, (block + 1) * out_rows), slice(tile * LANES, (tile + 1) * LANES))
                piece = field[(part,) + place] if part < 2 else (start if part == START else end)[place]
                own[base + tile * out_rows : base + (tile + 1) * out_rows, :] = piece

    for part in (END, START, RE, IM):
        block_own(part)
    pl.semaphore_wait(barrier, nd - 1 + nx - 1)
    for part in (END, START, RE, IM):
        for offset in far_first:
            bulk_copy(peer_at(offset), xr, part).start()

    if used_rows < LANES:
        for block in range(nx):
            for part in range(4):
                base = (block * 4 + part) * LANES
                pad = jnp.full((LANES - used_rows, LANES), 0.0 if part < 2 else 0.89, jnp.float32)
                received[base + used_rows : base + LANES, :] = pad
                own[base + used_rows : base + LANES, :] = pad
    for part in range(4):
        received[pl.ds(at(xr, part), used_rows), :] = own[pl.ds(at(xr, part), used_rows), :]

    def wide(ref, part, row):
        return jnp.concatenate(
            [ref[pl.ds((block * 4 + part) * LANES + row, slots, stride=out_rows), :] for block in range(nx)], axis=1
        )

    def cut(x, block):
        return cmap(lambda v: v[:, block * LANES : (block + 1) * LANES], x)

    coefs = [coefficient(depth_line, wide(own, START, row)) for row in range(out_rows)]
    forces = [(wide(own, RE, row), wide(own, IM, row)) for row in range(out_rows)]
    medium = segment_medium(depth_line, coefs)
    source = segment_source(depth_line, coefs, forces, medium[0], medium[2])
    mediums = [tuple(cut(v, block) for v in medium) for block in range(nx)]
    sources = [tuple(cut(v, block) for v in source) for block in range(nx)]
    total_medium, levels = medium_list(mediums)
    total_source, inners = source_list(levels, sources)
    for row, part in enumerate(v for pair in (*total_medium, *total_source) for v in pair):
        summary[pl.ds(row, slots, stride=SUMMARY_ROWS), :] = part

    def sum_copy(tile, origin):
        return pltpu.make_async_remote_copy(
            src_ref=summary.at[pl.ds(tile * SUMMARY_ROWS, SUMMARY_ROWS), :],
            dst_ref=gathered.at[pl.ds(pl.multiple_of(origin * SUMMARY_ROWS, SUMMARY_ROWS), SUMMARY_ROWS), :],
            send_sem=sum_send.at[tile],
            recv_sem=sum_recv.at[origin],
            device_id=(tile, xr),
            device_id_type=MESH,
        )

    for tile in range(tiles):

        @pl.when(dep != tile)
        def _():
            sum_copy(tile, dep).start()

    def ans_copy(peer, tile):
        return pltpu.make_async_remote_copy(
            src_ref=answer.at[pl.ds(pl.multiple_of(peer * SUBLANES, SUBLANES), SUBLANES), :],
            dst_ref=boundary.at[pl.ds(pl.multiple_of(tile * SUBLANES, SUBLANES), SUBLANES), :],
            send_sem=ans_send.at[peer],
            recv_sem=ans_recv.at[tile],
            device_id=(peer, xr),
            device_id_type=MESH,
        )

    if tiles < slots:
        boundary[tiles * SUBLANES :, :] = jnp.zeros(((slots - tiles) * SUBLANES, LANES), jnp.float32)

    @pl.when(dep < tiles)
    def _():
        gathered[pl.ds(pl.multiple_of(dep * SUMMARY_ROWS, SUMMARY_ROWS), SUMMARY_ROWS), :] = summary[
            pl.ds(pl.multiple_of(dep * SUMMARY_ROWS, SUMMARY_ROWS), SUMMARY_ROWS), :
        ]
        for offset in range(1, nd):
            sum_copy(0, lax.rem(dep + offset, nd)).wait_recv()
        values = [gathered[pl.ds(row, nd, stride=SUMMARY_ROWS), :] for row in range(10)]
        pairs = [(values[2 * i], values[2 * i + 1]) for i in range(5)]
        all_medium, all_levels = medium_tree(tuple(pairs[:3]), 0, nd)
        all_source, all_inners = source_tree(all_levels, tuple(pairs[3:]), 0)
        p_all, q_all = between_walls(depth_line, all_medium, all_source)
        p_all, q_all = down_tree(all_levels, all_inners, p_all, q_all, 0)
        for row, value in enumerate((*p_all, *q_all)):
            answer[pl.ds(row, nd, stride=SUBLANES), :] = value
        boundary[pl.ds(pl.multiple_of(dep * SUBLANES, SUBLANES), SUBLANES), :] = answer[pl.ds(pl.multiple_of(dep * SUBLANES, SUBLANES), SUBLANES), :]
        for offset in range(1, nd):
            ans_copy(lax.rem(dep + offset, nd), dep).start()

    for offset in range(nx):
        block = peer_at(offset)
        if offset > 0:
            bulk_copy(xr, block, END).wait_recv()
        tall_end[pl.ds(pl.multiple_of(block * LANES, LANES), LANES), :] = received[pl.ds(at(block, END), LANES), :].T
    cross_cells = LANES // SUBLANES

    def tall_strided(ref, *lead):
        return [
            jnp.concatenate(
                [
                    ref[lead + (pl.ds(block * LANES + cell, SUBLANES, stride=cross_cells), slice(None))]
                    for block in range(nx)
                ],
                axis=1,
            )
            for cell in range(cross_cells)
        ]

    def cross_coefs():
        return [coefficient(cross_line, v) for v in tall_strided(tall_end)]

    cross_medium = segment_medium(cross_line, cross_coefs())
    block_medium, block_levels = medium_tree(cross_medium, 0, SUBLANES)
    sub_place = lax.broadcasted_iota(jnp.int32, (SUBLANES, LANES), 0)
    lane_place = lax.broadcasted_iota(jnp.int32, (SUBLANES, LANES), 1)
    used = lane_place < tiles * out_rows

    def packed(value, fill):
        total = jnp.zeros((SUBLANES, LANES), jnp.float32)
        for block in range(nx):
            row = jnp.broadcast_to(value[0:1, block * LANES : (block + 1) * LANES], (SUBLANES, LANES))
            total = jnp.where(sub_place == block, row, total)
        return jnp.where(used, total, fill)

    def unpacked(value):
        return jnp.concatenate(
            [jnp.broadcast_to(value[block : block + 1, :], (SUBLANES, LANES)) for block in range(nx)], axis=1
        )

    packed_medium = tuple(
        (packed(v[0], fill), packed(v[1], 0.0)) for v, fill in zip(block_medium, (1.0, 0.0, 0.0))
    )
    tile_medium, tile_levels = medium_tree(packed_medium, 1, slots, out_rows)
    line_medium, line_levels = medium_tree(tile_medium, 0, nx)

    for tile in range(tiles):

        @pl.when(dep != tile)
        def _():
            ans_copy(dep, tile).wait_recv()

    edge_rows = 4 * slots
    incoming = [boundary[pl.ds(row, slots, stride=SUBLANES), :] for row in range(4)]
    waves = down_list(levels, inners, (incoming[0], incoming[1]), (incoming[2], incoming[3]))
    for block, (p_left, q_right) in enumerate(waves):
        before, here = segment_start(depth_line, mediums[block], sources[block], p_left, q_right)
        for row, value in enumerate((*before, *here)):
            first = block * edge_rows + row * slots
            edge_out[first : first + slots, :] = value

    def edge_at(block):
        return pl.ds(pl.multiple_of(block * edge_rows, edge_rows), edge_rows)

    def edge_copy(peer, source_block):
        return pltpu.make_async_remote_copy(
            src_ref=edge_out.at[edge_at(peer), :],
            dst_ref=edge_in.at[edge_at(source_block), :],
            send_sem=edge_send.at[peer],
            recv_sem=edge_recv.at[source_block],
            device_id=(dep, peer),
            device_id_type=MESH,
        )

    for offset in far_first:
        edge_copy(peer_at(offset), xr).start()
    edge_in[edge_at(xr), :] = edge_out[edge_at(xr), :]

    for group in range(0, nx, 2):
        blocks = [peer_at(group), peer_at(group + 1)]
        for offset, block in enumerate(blocks, group):
            if offset > 0:
                for part in (START, RE, IM):
                    bulk_copy(xr, block, part).wait_recv()
                edge_copy(xr, block).wait_recv()

        def side(ref, first, **keywords):
            return jnp.concatenate([ref[pl.ds(first(block), slots, **keywords), :] for block in blocks], axis=1)

        def row_of(part, row):
            return side(received, lambda block: at(block, part) + row, stride=out_rows)

        def edge_of(row):
            return side(edge_in, lambda block: pl.multiple_of(block * edge_rows + row * slots, SUBLANES))

        before, here = (edge_of(0), edge_of(1)), (edge_of(2), edge_of(3))
        for row in range(out_rows):
            force = (row_of(RE, row), row_of(IM, row))
            value = result(depth_line, force, here)
            for c in range(2):
                for side_at in range(2):
                    place = pl.ds((side_at * 2 + c) * LANES + row, slots, stride=out_rows)
                    middle[place, :] = value[c][:, side_at * LANES : (side_at + 1) * LANES]
            if row < out_rows - 1:
                coef = coefficient(depth_line, row_of(START, row))
                before, here = here, step(depth_line, coef, here, before, force)
        for side_at, block in enumerate(blocks):
            for c in range(2):
                first = (side_at * 2 + c) * LANES
                tall_field[c, pl.ds(pl.multiple_of(block * LANES, LANES), LANES), :] = middle[first : first + LANES, :].T

    coefs = cross_coefs()
    forces = list(zip(tall_strided(tall_field, 0), tall_strided(tall_field, 1)))
    source = segment_source(cross_line, coefs, forces, cross_medium[0], cross_medium[2])
    block_source, block_inners = source_tree(block_levels, source, 0)
    packed_source = tuple((packed(v[0], 0.0), packed(v[1], 0.0)) for v in block_source)
    tile_source, tile_inners = source_tree(tile_levels, packed_source, 1)
    line_source, line_inners = source_tree(line_levels, tile_source, 0)
    p_left, q_right = between_walls(cross_line, line_medium, line_source)
    p_left, q_right = down_tree(line_levels, line_inners, p_left, q_right, 0)
    p_left, q_right = down_tree(tile_levels, tile_inners, p_left, q_right, 1)
    p_left, q_right = cmap(unpacked, p_left), cmap(unpacked, q_right)
    p_left, q_right = down_tree(block_levels, block_inners, p_left, q_right, 0)
    all_before, all_here = segment_start(cross_line, cross_medium, source, p_left, q_right)
    for block in range(nx):
        before, here = cut(all_before, block), cut(all_here, block)
        for cell in range(cross_cells):
            place = pl.ds(block * LANES + cell, SUBLANES, stride=cross_cells)
            force = (tall_field[0, place, :], tall_field[1, place, :])
            value = result(cross_line, force, here)
            tall_out[0, place, :] = value[0]
            tall_out[1, place, :] = value[1]
            if cell < cross_cells - 1:
                coef = coefficient(cross_line, tall_end[place, :])
                before, here = here, step(cross_line, coef, here, before, force)
        for c in range(2):
            flat = tall_out[c, block * LANES : (block + 1) * LANES, :].T
            for tile in range(tiles):
                first = block * width + tile * LANES
                out[c, :, first : first + LANES] = flat[tile * out_rows : (tile + 1) * out_rows, :]

    for offset in range(1, nx):
        peer = peer_at(offset)
        edge_copy(peer, xr).wait_send()
        for part in range(4):
            bulk_copy(peer, xr, part).wait_send()
    for tile in range(tiles):

        @pl.when(dep != tile)
        def _():
            sum_copy(tile, dep).wait_send()

    @pl.when(dep < tiles)
    def _():
        for offset in range(1, nd):
            ans_copy(lax.rem(dep + offset, nd), dep).wait_send()


def local(nd, nx, sound_field, index_start, index_end):
    rows, width = index_start.shape
    tiles = width // LANES
    out_rows = rows // nx
    slots = LANES // out_rows
    assert tiles <= nd and tiles <= slots and slots == SUBLANES and nx <= SUBLANES and nx % 2 == 0

    f32 = jnp.float32
    dma = pltpu.SemaphoreType.DMA
    return pl.pallas_call(
        functools.partial(kernel, nd, nx),
        out_shape=jax.ShapeDtypeStruct((2, out_rows, width * nx), f32),
        in_specs=[pl.BlockSpec(memory_space=pltpu.VMEM)] * 3,
        out_specs=pl.BlockSpec(memory_space=pltpu.VMEM),
        scratch_shapes=[
            pltpu.VMEM((nx * 4 * LANES, LANES), f32),
            pltpu.VMEM((nx * 4 * LANES, LANES), f32),
            pltpu.VMEM((slots * SUMMARY_ROWS, LANES), f32),
            pltpu.VMEM((nd * SUMMARY_ROWS, LANES), f32),
            pltpu.VMEM((nd * SUBLANES, LANES), f32),
            pltpu.VMEM((slots * SUBLANES, LANES), f32),
            pltpu.VMEM((nx * 4 * slots, LANES), f32),
            pltpu.VMEM((nx * 4 * slots, LANES), f32),
            pltpu.VMEM((4 * LANES, LANES), f32),
            pltpu.VMEM((nx * LANES, LANES), f32),
            pltpu.VMEM((2, nx * LANES, LANES), f32),
            pltpu.VMEM((2, nx * LANES, LANES), f32),
            dma((tiles,)),
            dma((nd,)),
            dma((nd,)),
            dma((tiles,)),
            dma((nx, 4)),
            dma((nx, 4)),
            dma((nx,)),
            dma((nx,)),
        ],
        compiler_params=pltpu.CompilerParams(
            collective_id=0, has_side_effects=True, vmem_limit_bytes=32 * 1024 * 1024
        ),
        cost_estimate=pl.CostEstimate(flops=20_000_000, bytes_accessed=2_000_000, transcendentals=0),
    )(sound_field, index_start, index_end)


def solution(mesh):
    nd, nx = mesh.shape["depth"], mesh.shape["xr"]
    in_specs = (P(None, "depth", "xr"), P("depth", "xr"), P("depth", "xr"))
    out_specs = P(None, ("depth", "xr"), None)
    return jax.shard_map(
        functools.partial(local, nd, nx), mesh=mesh, in_specs=in_specs, out_specs=out_specs, check_vma=False
    )
```

```python
import functools

import jax
import jax.numpy as jnp
from jax import lax
from jax.experimental import pallas as pl
from jax.experimental.pallas import tpu as pltpu
from jax.sharding import PartitionSpec as P
import numpy as np

depth_stiffness = 1.6
cross_stiffness = 1.2
numer = 2.857 + 0.004j
denom = 2.857 - 0.004j
LANES = 128
SUBLANES = 8
SUMMARY_ROWS = 16
MESH = pl.DeviceIdType.MESH


class Line:
    def __init__(self, stiffness):
        shift = 1.0 / denom
        self.slope = -0.5 / stiffness
        self.level = 2.0 - shift.real / stiffness + 0.5 / stiffness
        self.damping = shift.imag / stiffness
        cosine = 0.5 * (self.level + self.slope * 0.89)
        angle = float(np.arccos(cosine))
        self.mu = complex(np.exp(0.5j * angle))
        self.nu = self.mu.conjugate()
        self.inv_det = 1.0 / (self.nu * self.nu - self.mu * self.mu)
        self.wall = -self.mu * self.mu
        self.alpha = numer / denom
        self.beta = (denom - numer) / (denom * denom * stiffness)


def mul(x, y):
    return (x[0] * y[0] - x[1] * y[1], x[0] * y[1] + x[1] * y[0])


def add(x, y):
    return (x[0] + y[0], x[1] + y[1])


def sub(x, y):
    return (x[0] - y[0], x[1] - y[1])


def cmul(c, x):
    c = complex(c)
    return (c.real * x[0] - c.imag * x[1], c.real * x[1] + c.imag * x[0])


def recip(x):
    scale = 1.0 / (x[0] * x[0] + x[1] * x[1])
    return (x[0] * scale, -x[1] * scale)


def one_minus(x):
    return (1.0 - x[0], -x[1])


def cmap(fn, x):
    return (fn(x[0]), fn(x[1]))


def step(line, coef, here, before, force=None):
    real = coef * here[0] + line.damping * here[1] - before[0]
    imag = coef * here[1] - line.damping * here[0] - before[1]
    if force is not None:
        real, imag = real + force[0], imag + force[1]
    return (real, imag)


def coefficient(line, index):
    return line.level + line.slope * index


def segment_medium(line, coefs):
    shape = coefs[0].shape
    def const(c):
        return (jnp.full(shape, c.real, jnp.float32), jnp.full(shape, c.imag, jnp.float32))
    p0, p1 = const(line.nu), const(line.mu)
    q0, q1 = const(line.mu), const(line.nu)
    for coef in coefs:
        p0, p1 = p1, step(line, coef, p1, p0)
        q0, q1 = q1, step(line, coef, q1, q0)
    lower, upper = -line.mu * line.inv_det, line.nu * line.inv_det
    t21 = add(cmul(lower, p0), cmul(upper, p1))
    t22 = add(cmul(lower, q0), cmul(upper, q1))
    t12 = add(cmul(upper, q0), cmul(lower, q1))
    t = recip(t22)
    r1 = mul(t21, t)
    r1 = (-r1[0], -r1[1])
    r2 = mul(t12, t)
    return t, r1, r2


def segment_source(line, coefs, forces, t, r2):
    zero = jnp.zeros(coefs[0].shape, jnp.float32)
    v0, v1 = (zero, zero), (zero, zero)
    for position, (coef, force) in enumerate(zip(coefs, forces)):
        if position == 0:
            v0, v1 = v1, force
        else:
            v0, v1 = v1, step(line, coef, v1, v0, force)
    lower, upper = -line.mu * line.inv_det, line.nu * line.inv_det
    right = add(cmul(upper, v0), cmul(lower, v1))
    left = add(cmul(lower, v0), cmul(upper, v1))
    s1 = mul(left, t)
    s1 = (-s1[0], -s1[1])
    s2 = sub(right, mul(r2, left))
    return s1, s2


def from_right(x, axis, amount):
    return cmap(lambda v: pltpu.roll(v, v.shape[axis] - amount, axis), x)


def from_left(x, axis, amount):
    return cmap(lambda v: pltpu.roll(v, amount, axis), x)


def merge_medium(left, right):
    t_a, r1_a, r2_a = left
    t_b, r1_b, r2_b = right
    d = recip(one_minus(mul(r2_a, r1_b)))
    ra, rb = mul(d, r2_a), mul(d, r1_b)
    tad, tbd = mul(t_a, d), mul(t_b, d)
    x1, x2 = mul(t_a, rb), mul(t_b, ra)
    merged = (mul(tad, t_b), add(r1_a, mul(x1, t_a)), add(r2_b, mul(x2, t_b)))
    return merged, (d, ra, rb, t_a, t_b, tad, tbd, x1, x2)


def merge_source(kept, left, right):
    d, ra, rb, t_a, t_b, tad, tbd, x1, x2 = kept
    s1_a, s2_a = left
    s1_b, s2_b = right
    e_p = add(mul(d, s2_a), mul(ra, s1_b))
    e_q = add(mul(d, s1_b), mul(rb, s2_a))
    merged = (add(s1_a, mul(t_a, e_q)), add(s2_b, mul(t_b, e_p)))
    return merged, (e_p, e_q)


def middle_waves(kept, inner, p_left, q_right):
    d, ra, rb, t_a, t_b, tad, tbd, x1, x2 = kept
    p_mid = add(add(mul(tad, p_left), mul(x2, q_right)), inner[0])
    q_mid = add(add(mul(x1, p_left), mul(tbd, q_right)), inner[1])
    return p_mid, q_mid


def medium_list(items):
    levels = []
    while len(items) > 1:
        pairs = [merge_medium(a, b) for a, b in zip(items[0::2], items[1::2])]
        items = [merged for merged, _ in pairs]
        levels.append([kept for _, kept in pairs])
    return items[0], levels


def source_list(levels, items):
    inners = []
    for level in levels:
        pairs = [merge_source(kept, a, b) for kept, a, b in zip(level, items[0::2], items[1::2])]
        items = [merged for merged, _ in pairs]
        inners.append([inner for _, inner in pairs])
    return items[0], inners


def down_list(levels, inners, p_left, q_right):
    waves = [(p_left, q_right)]
    for level, inner_level in zip(reversed(levels), reversed(inners)):
        finer = []
        for kept, inner, (p, q) in zip(level, inner_level, waves):
            p_mid, q_mid = middle_waves(kept, inner, p, q)
            finer += [(p, q_mid), (p_mid, q)]
        waves = finer
    return waves


def medium_level(medium, axis, amount):
    return merge_medium(medium, tuple(from_right(v, axis, amount) for v in medium))


def source_level(kept, source, axis, amount):
    return merge_source(kept, source, tuple(from_right(v, axis, amount) for v in source))


def down_level(kept, inner, p_left, q_right, axis, amount):
    p_mid, q_mid = middle_waves(kept, inner, p_left, q_right)
    shape = p_left[0].shape
    place = lax.broadcasted_iota(jnp.int32, shape, axis)
    is_left = (place % (2 * amount)) < amount
    p_moved = from_left(p_mid, axis, amount)
    q_moved = from_left(q_right, axis, amount)
    p_new = tuple(jnp.where(is_left, a, b) for a, b in zip(p_left, p_moved))
    q_new = tuple(jnp.where(is_left, a, b) for a, b in zip(q_mid, q_moved))
    return p_new, q_new


def medium_tree(medium, axis, count, unit=1):
    levels = []
    amount = unit
    while amount < count * unit:
        medium, kept = medium_level(medium, axis, amount)
        levels.append((amount, kept))
        amount *= 2
    return medium, levels


def source_tree(levels, source, axis):
    inners = []
    for amount, kept in levels:
        source, inner = source_level(kept, source, axis, amount)
        inners.append(inner)
    return source, inners


def down_tree(levels, inners, p_left, q_right, axis):
    for (amount, kept), inner in zip(reversed(levels), reversed(inners)):
        p_left, q_right = down_level(kept, inner, p_left, q_right, axis, amount)
    return p_left, q_right


def between_walls(line, medium, source):
    t, r1, r2 = medium
    s1, s2 = source
    tw = cmul(line.wall, t)
    first = one_minus(cmul(line.wall, r1))
    second = one_minus(cmul(line.wall, r2))
    scale = recip(sub(mul(first, second), mul(tw, tw)))
    q_left = mul(scale, add(mul(second, s1), mul(tw, s2)))
    p_right = mul(scale, add(mul(tw, s1), mul(first, s2)))
    return cmul(line.wall, q_left), cmul(line.wall, p_right)


def segment_start(line, medium, source, p_left, q_right):
    t, r1, r2 = medium
    q_left = add(add(mul(r1, p_left), mul(t, q_right)), source[0])
    before = add(cmul(line.nu, p_left), cmul(line.mu, q_left))
    here = add(cmul(line.mu, p_left), cmul(line.nu, q_left))
    return before, here


def result(line, force, here):
    return add(cmul(line.alpha, force), cmul(line.beta, here))


def kernel(
    nd, nx, field, start, end, out,
    own, received, summary, gathered, answer, boundary, edge_out, edge_in,
    middle, tall_end, tall_field, tall_out,
    sum_send, sum_recv, ans_send, ans_recv, bulk_send, bulk_recv, edge_send, edge_recv,
):
    width = out.shape[2] // nx
    tiles = width // LANES
    out_rows = out.shape[1]
    used_rows = tiles * out_rows
    slots = LANES // out_rows
    dep = lax.axis_index("depth")
    xr = lax.axis_index("xr")
    depth_line = Line(depth_stiffness)
    cross_line = Line(cross_stiffness)

    barrier = pltpu.get_barrier_semaphore()

    @pl.loop(1, nd)
    def _(offset):
        pl.semaphore_signal(barrier, 1, device_id=(lax.rem(dep + offset, nd), xr), device_id_type=MESH)

    @pl.loop(1, nx)
    def _(offset):
        pl.semaphore_signal(barrier, 1, device_id=(dep, lax.rem(xr + offset, nx)), device_id_type=MESH)

    def peer_at(offset):
        base = xr // 2 * 2
        return lax.rem(base + 2 * (offset // 2), nx) + lax.rem(xr + offset, 2)

    RE, IM, START, END = range(4)

    def at(block, part):
        return pl.multiple_of((block * 4 + part) * LANES, LANES)

    def bulk_copy(peer, source_block, part):
        return pltpu.make_async_remote_copy(
            src_ref=own.at[pl.ds(at(peer, part), used_rows), :],
            dst_ref=received.at[pl.ds(at(source_block, part), used_rows), :],
            send_sem=bulk_send.at[peer, part],
            recv_sem=bulk_recv.at[source_block, part],
            device_id=(dep, peer),
            device_id_type=MESH,
        )

    far_first = list(range(2, nx)) + [1]

    def block_own(part):
        for block in range(nx):
            base = (block * 4 + part) * LANES
            for tile in range(tiles):
                place = slice(block * out_rows, (block + 1) * out_rows)
                piece = field[tile, part, place] if part < 2 else (start if part == START else end)[tile, place]
                own[base + tile * out_rows : base + (tile + 1) * out_rows, :] = piece

    for part in (END, START, RE, IM):
        block_own(part)
    pl.semaphore_wait(barrier, nd - 1 + nx - 1)
    for part in (END, START, RE, IM):
        for offset in far_first:
            bulk_copy(peer_at(offset), xr, part).start()

    if used_rows < LANES:
        for block in range(nx):
            for part in range(4):
                base = (block * 4 + part) * LANES
                pad = jnp.full((LANES - used_rows, LANES), 0.0 if part < 2 else 0.89, jnp.float32)
                received[base + used_rows : base + LANES, :] = pad
                own[base + used_rows : base + LANES, :] = pad
    for part in range(4):
        received[pl.ds(at(xr, part), used_rows), :] = own[pl.ds(at(xr, part), used_rows), :]

    def wide(ref, part, row):
        return jnp.concatenate(
            [ref[pl.ds((block * 4 + part) * LANES + row, slots, stride=out_rows), :] for block in range(nx)], axis=1
        )

    def cut(x, block):
        return cmap(lambda v: v[:, block * LANES : (block + 1) * LANES], x)

    coefs = [coefficient(depth_line, wide(own, START, row)) for row in range(out_rows)]
    forces = [(wide(own, RE, row), wide(own, IM, row)) for row in range(out_rows)]
    medium = segment_medium(depth_line, coefs)
    source = segment_source(depth_line, coefs, forces, medium[0], medium[2])
    mediums = [tuple(cut(v, block) for v in medium) for block in range(nx)]
    sources = [tuple(cut(v, block) for v in source) for block in range(nx)]
    total_medium, levels = medium_list(mediums)
    total_source, inners = source_list(levels, sources)
    for row, part in enumerate(v for pair in (*total_medium, *total_source) for v in pair):
        summary[pl.ds(row, slots, stride=SUMMARY_ROWS), :] = part

    def sum_copy(tile, origin):
        return pltpu.make_async_remote_copy(
            src_ref=summary.at[pl.ds(tile * SUMMARY_ROWS, SUMMARY_ROWS), :],
            dst_ref=gathered.at[pl.ds(pl.multiple_of(origin * SUMMARY_ROWS, SUMMARY_ROWS), SUMMARY_ROWS), :],
            send_sem=sum_send.at[tile],
            recv_sem=sum_recv.at[origin],
            device_id=(tile, xr),
            device_id_type=MESH,
        )

    for tile in range(tiles):

        @pl.when(dep != tile)
        def _():
            sum_copy(tile, dep).start()

    def ans_copy(peer, tile):
        return pltpu.make_async_remote_copy(
            src_ref=answer.at[pl.ds(pl.multiple_of(peer * SUBLANES, SUBLANES), SUBLANES), :],
            dst_ref=boundary.at[pl.ds(pl.multiple_of(tile * SUBLANES, SUBLANES), SUBLANES), :],
            send_sem=ans_send.at[peer],
            recv_sem=ans_recv.at[tile],
            device_id=(peer, xr),
            device_id_type=MESH,
        )

    if tiles < slots:
        boundary[tiles * SUBLANES :, :] = jnp.zeros(((slots - tiles) * SUBLANES, LANES), jnp.float32)

    @pl.when(dep < tiles)
    def _():
        gathered[pl.ds(pl.multiple_of(dep * SUMMARY_ROWS, SUMMARY_ROWS), SUMMARY_ROWS), :] = summary[
            pl.ds(pl.multiple_of(dep * SUMMARY_ROWS, SUMMARY_ROWS), SUMMARY_ROWS), :
        ]
        for offset in range(1, nd):
            sum_copy(0, lax.rem(dep + offset, nd)).wait_recv()
        values = [gathered[pl.ds(row, nd, stride=SUMMARY_ROWS), :] for row in range(10)]
        pairs = [(values[2 * i], values[2 * i + 1]) for i in range(5)]
        all_medium, all_levels = medium_tree(tuple(pairs[:3]), 0, nd)
        all_source, all_inners = source_tree(all_levels, tuple(pairs[3:]), 0)
        p_all, q_all = between_walls(depth_line, all_medium, all_source)
        p_all, q_all = down_tree(all_levels, all_inners, p_all, q_all, 0)
        for row, value in enumerate((*p_all, *q_all)):
            answer[pl.ds(row, nd, stride=SUBLANES), :] = value
        boundary[pl.ds(pl.multiple_of(dep * SUBLANES, SUBLANES), SUBLANES), :] = answer[pl.ds(pl.multiple_of(dep * SUBLANES, SUBLANES), SUBLANES), :]
        for offset in range(1, nd):
            ans_copy(lax.rem(dep + offset, nd), dep).start()

    for offset in range(nx):
        block = peer_at(offset)
        if offset > 0:
            bulk_copy(xr, block, END).wait_recv()
        tall_end[pl.ds(pl.multiple_of(block * LANES, LANES), LANES), :] = received[pl.ds(at(block, END), LANES), :].T
    cross_cells = LANES // SUBLANES

    def tall_strided(ref, *lead):
        return [
            jnp.concatenate(
                [
                    ref[lead + (pl.ds(block * LANES + cell, SUBLANES, stride=cross_cells), slice(None))]
                    for block in range(nx)
                ],
                axis=1,
            )
            for cell in range(cross_cells)
        ]

    def cross_coefs():
        return [coefficient(cross_line, v) for v in tall_strided(tall_end)]

    cross_medium = segment_medium(cross_line, cross_coefs())
    block_medium, block_levels = medium_tree(cross_medium, 0, SUBLANES)
    sub_place = lax.broadcasted_iota(jnp.int32, (SUBLANES, LANES), 0)
    lane_place = lax.broadcasted_iota(jnp.int32, (SUBLANES, LANES), 1)
    used = lane_place < tiles * out_rows

    def packed(value, fill):
        total = jnp.zeros((SUBLANES, LANES), jnp.float32)
        for block in range(nx):
            row = jnp.broadcast_to(value[0:1, block * LANES : (block + 1) * LANES], (SUBLANES, LANES))
            total = jnp.where(sub_place == block, row, total)
        return jnp.where(used, total, fill)

    def unpacked(value):
        return jnp.concatenate(
            [jnp.broadcast_to(value[block : block + 1, :], (SUBLANES, LANES)) for block in range(nx)], axis=1
        )

    packed_medium = tuple(
        (packed(v[0], fill), packed(v[1], 0.0)) for v, fill in zip(block_medium, (1.0, 0.0, 0.0))
    )
    tile_medium, tile_levels = medium_tree(packed_medium, 1, slots, out_rows)
    line_medium, line_levels = medium_tree(tile_medium, 0, nx)

    for tile in range(tiles):

        @pl.when(dep != tile)
        def _():
            ans_copy(dep, tile).wait_recv()

    edge_rows = 4 * slots
    incoming = [boundary[pl.ds(row, slots, stride=SUBLANES), :] for row in range(4)]
    waves = down_list(levels, inners, (incoming[0], incoming[1]), (incoming[2], incoming[3]))
    for block, (p_left, q_right) in enumerate(waves):
        before, here = segment_start(depth_line, mediums[block], sources[block], p_left, q_right)
        for row, value in enumerate((*before, *here)):
            first = block * edge_rows + row * slots
            edge_out[first : first + slots, :] = value

    def edge_at(block):
        return pl.ds(pl.multiple_of(block * edge_rows, edge_rows), edge_rows)

    def edge_copy(peer, source_block):
        return pltpu.make_async_remote_copy(
            src_ref=edge_out.at[edge_at(peer), :],
            dst_ref=edge_in.at[edge_at(source_block), :],
            send_sem=edge_send.at[peer],
            recv_sem=edge_recv.at[source_block],
            device_id=(dep, peer),
            device_id_type=MESH,
        )

    for offset in far_first:
        edge_copy(peer_at(offset), xr).start()
    edge_in[edge_at(xr), :] = edge_out[edge_at(xr), :]

    for group in range(0, nx, 2):
        blocks = [peer_at(group), peer_at(group + 1)]
        for offset, block in enumerate(blocks, group):
            if offset > 0:
                for part in (START, RE, IM):
                    bulk_copy(xr, block, part).wait_recv()
                edge_copy(xr, block).wait_recv()

        def side(ref, first, **keywords):
            return jnp.concatenate([ref[pl.ds(first(block), slots, **keywords), :] for block in blocks], axis=1)

        def row_of(part, row):
            return side(received, lambda block: at(block, part) + row, stride=out_rows)

        def edge_of(row):
            return side(edge_in, lambda block: pl.multiple_of(block * edge_rows + row * slots, SUBLANES))

        before, here = (edge_of(0), edge_of(1)), (edge_of(2), edge_of(3))
        for row in range(out_rows):
            force = (row_of(RE, row), row_of(IM, row))
            value = result(depth_line, force, here)
            for c in range(2):
                for side_at in range(2):
                    place = pl.ds((side_at * 2 + c) * LANES + row, slots, stride=out_rows)
                    middle[place, :] = value[c][:, side_at * LANES : (side_at + 1) * LANES]
            if row < out_rows - 1:
                coef = coefficient(depth_line, row_of(START, row))
                before, here = here, step(depth_line, coef, here, before, force)
        for side_at, block in enumerate(blocks):
            for c in range(2):
                first = (side_at * 2 + c) * LANES
                tall_field[c, pl.ds(pl.multiple_of(block * LANES, LANES), LANES), :] = middle[first : first + LANES, :].T

    coefs = cross_coefs()
    forces = list(zip(tall_strided(tall_field, 0), tall_strided(tall_field, 1)))
    source = segment_source(cross_line, coefs, forces, cross_medium[0], cross_medium[2])
    block_source, block_inners = source_tree(block_levels, source, 0)
    packed_source = tuple((packed(v[0], 0.0), packed(v[1], 0.0)) for v in block_source)
    tile_source, tile_inners = source_tree(tile_levels, packed_source, 1)
    line_source, line_inners = source_tree(line_levels, tile_source, 0)
    p_left, q_right = between_walls(cross_line, line_medium, line_source)
    p_left, q_right = down_tree(line_levels, line_inners, p_left, q_right, 0)
    p_left, q_right = down_tree(tile_levels, tile_inners, p_left, q_right, 1)
    p_left, q_right = cmap(unpacked, p_left), cmap(unpacked, q_right)
    p_left, q_right = down_tree(block_levels, block_inners, p_left, q_right, 0)
    all_before, all_here = segment_start(cross_line, cross_medium, source, p_left, q_right)
    for block in range(nx):
        before, here = cut(all_before, block), cut(all_here, block)
        for cell in range(cross_cells):
            place = pl.ds(block * LANES + cell, SUBLANES, stride=cross_cells)
            force = (tall_field[0, place, :], tall_field[1, place, :])
            value = result(cross_line, force, here)
            tall_out[0, place, :] = value[0]
            tall_out[1, place, :] = value[1]
            if cell < cross_cells - 1:
                coef = coefficient(cross_line, tall_end[place, :])
                before, here = here, step(cross_line, coef, here, before, force)
        for c in range(2):
            flat = tall_out[c, block * LANES : (block + 1) * LANES, :].T
            for tile in range(tiles):
                first = block * width + tile * LANES
                out[c, :, first : first + LANES] = flat[tile * out_rows : (tile + 1) * out_rows, :]

    for offset in range(1, nx):
        peer = peer_at(offset)
        edge_copy(peer, xr).wait_send()
        for part in range(4):
            bulk_copy(peer, xr, part).wait_send()
    for tile in range(tiles):

        @pl.when(dep != tile)
        def _():
            sum_copy(tile, dep).wait_send()

    @pl.when(dep < tiles)
    def _():
        for offset in range(1, nd):
            ans_copy(lax.rem(dep + offset, nd), dep).wait_send()


def local(nd, nx, sound_field, index_start, index_end):
    rows, width = index_start.shape
    tiles = width // LANES
    out_rows = rows // nx
    slots = LANES // out_rows
    assert tiles <= nd and tiles <= slots and slots == SUBLANES and nx <= SUBLANES and nx % 2 == 0

    field = sound_field.reshape(2, rows, tiles, LANES).transpose(2, 0, 1, 3)
    start = index_start.reshape(rows, tiles, LANES).transpose(1, 0, 2)
    end = index_end.reshape(rows, tiles, LANES).transpose(1, 0, 2)
    f32 = jnp.float32
    dma = pltpu.SemaphoreType.DMA
    return pl.pallas_call(
        functools.partial(kernel, nd, nx),
        out_shape=jax.ShapeDtypeStruct((2, out_rows, width * nx), f32),
        in_specs=[pl.BlockSpec(memory_space=pltpu.VMEM)] * 3,
        out_specs=pl.BlockSpec(memory_space=pltpu.VMEM),
        scratch_shapes=[
            pltpu.VMEM((nx * 4 * LANES, LANES), f32),
            pltpu.VMEM((nx * 4 * LANES, LANES), f32),
            pltpu.VMEM((slots * SUMMARY_ROWS, LANES), f32),
            pltpu.VMEM((nd * SUMMARY_ROWS, LANES), f32),
            pltpu.VMEM((nd * SUBLANES, LANES), f32),
            pltpu.VMEM((slots * SUBLANES, LANES), f32),
            pltpu.VMEM((nx * 4 * slots, LANES), f32),
            pltpu.VMEM((nx * 4 * slots, LANES), f32),
            pltpu.VMEM((4 * LANES, LANES), f32),
            pltpu.VMEM((nx * LANES, LANES), f32),
            pltpu.VMEM((2, nx * LANES, LANES), f32),
            pltpu.VMEM((2, nx * LANES, LANES), f32),
            dma((tiles,)),
            dma((nd,)),
            dma((nd,)),
            dma((tiles,)),
            dma((nx, 4)),
            dma((nx, 4)),
            dma((nx,)),
            dma((nx,)),
        ],
        compiler_params=pltpu.CompilerParams(
            collective_id=0, has_side_effects=True, vmem_limit_bytes=32 * 1024 * 1024
        ),
        cost_estimate=pl.CostEstimate(flops=20_000_000, bytes_accessed=2_000_000, transcendentals=0),
    )(field, start, end)


def solution(mesh):
    nd, nx = mesh.shape["depth"], mesh.shape["xr"]
    in_specs = (P(None, "depth", "xr"), P("depth", "xr"), P("depth", "xr"))
    out_specs = P(None, ("depth", "xr"), None)
    return jax.shard_map(
        functools.partial(local, nd, nx), mesh=mesh, in_specs=in_specs, out_specs=out_specs, check_vma=False
    )
```
